128 devices in a mesh: gy: 16 (over x, y_lo, core), gx: 8 (over y_hi, z).
Axes of the slice: x: 4, y: 4 (y_hi: 2, y_lo: 2; y = y_hi * 2 + y_lo), z: 4, core: 2. Of those that a mesh axis runs over, the one named last changes fastest.
Arguments:
- tokens: bfloat16 [256, 512, 512], P('gy', 'gx'), may hold values from -6 to 6
- cotangent: bfloat16 [256, 512, 512], P('gy', 'gx'), may hold values from -6 to 6
- w_qkv: bfloat16 [512, 1536], replicated, may hold values from -0.25 to 0.25
- w_out: bfloat16 [512, 512], replicated, may hold values from -0.25 to 0.25
Outputs:
- grad_tokens: bfloat16 [256, 512, 512], P('gy', 'gx')
- grad_wqkv: float32 [512, 1536], P(('gy', 'gx'))
- grad_wout: float32 [512, 512], P(('gy', 'gx'))
The draws below stay inside these ranges and needn't reach their ends.
All inputs are finite; a program needn't handle non-finite values.
Results may differ from the reference program's by a relative error of at most 0.0095.
Values may be sent and summed in bfloat16 or wider, within the bound.
A program may use at most 128 MiB of HBM per device.

```python
import jax
import jax.numpy as jnp
from jax import lax

D = 512
HEADS = 16
GRID = 8
H = 256
W = 512
TOKENS = 131072


def level_of(rng, extent, split, low, largest):
    def one(position, shards_of):
        steps = jax.random.uniform(jax.random.fold_in(jax.random.fold_in(rng, 6), position), (shards_of,), jnp.float32, low / len(split), largest / len(split))
        return jnp.repeat(jnp.exp(steps), extent[position] // shards_of).reshape((-1,) + (1,) * (len(extent) - position - 1))

    loudness = one(*split[0])
    for cut in split[1:]:
        loudness = loudness * one(*cut)
    return loudness


def bell_draw(key, dims, scale, limit, shards=(), kind=jnp.bfloat16):
    values = scale * jax.random.normal(key, dims, jnp.float32)
    if shards:
        values = values * level_of(key, dims, shards, -0.22, 0.18)
    return jnp.clip(values, -limit, limit).astype(kind)


def setup_inputs(seed: int = 0) -> dict:
    seeds = jax.random.split(jax.random.key(seed), 5)
    return {
        "tokens": bell_draw(seeds[0], (H, W, D), 1.0, 6.0, ((0, 16), (1, 8))),
        "cotangent": bell_draw(seeds[1], (H, W, D), 1.0, 6.0, ((0, 16), (1, 8))),
        "w_qkv": bell_draw(seeds[2], (D, 3 * D), D ** -0.5, 0.25),
        "w_out": bell_draw(seeds[3], (D, D), D ** -0.5, 0.25),
    }


EPS = 1e-05

def window_pass(token_win, cot_win, w_qkv, w_out):
    windows, members, channels = token_win.shape
    head_size = channels // HEADS
    score_scale = head_size ** (-0.5)
    values_f = token_win.astype(jnp.float32)
    average = lax.optimization_barrier(jnp.mean(values_f, axis=-1, keepdims=True))
    centred_input = values_f - average
    variance = lax.optimization_barrier(jnp.mean(centred_input * centred_input, axis=-1, keepdims=True))
    inverse_deviation = lax.rsqrt(variance + EPS)
    standardized_input = centred_input * inverse_deviation
    normalized_tokens = standardized_input.astype(jnp.bfloat16)
    qkv = jnp.dot(normalized_tokens.reshape(-1, channels), w_qkv, preferred_element_type=jnp.float32)
    qkv = qkv.astype(jnp.bfloat16).reshape(windows, members, 3, HEADS, head_size)
    query = qkv[:, :, 0].astype(jnp.float32)
    keys_f = qkv[:, :, 1].astype(jnp.float32)
    value_f = qkv[:, :, 2].astype(jnp.float32)
    scores = jnp.einsum('bqhe,bkhe->bhqk', query, keys_f) * score_scale
    exponent = jnp.exp(scores)
    softmax = exponent / lax.optimization_barrier(jnp.sum(exponent, axis=-1, keepdims=True))
    soft_low = softmax.astype(jnp.bfloat16)
    attended = jnp.einsum('bhqk,bkhe->bqhe', soft_low.astype(jnp.float32), value_f).astype(jnp.bfloat16)
    grad_att = jnp.dot(cot_win.reshape(-1, channels), w_out.T, preferred_element_type=jnp.float32)
    grad_att = grad_att.astype(jnp.bfloat16).reshape(windows, members, HEADS, head_size)
    grad_att_f = grad_att.astype(jnp.float32)
    grad_probs = jnp.einsum('bqhe,bkhe->bhqk', grad_att_f, value_f)
    grad_scores = softmax * (grad_probs - lax.optimization_barrier(jnp.sum(softmax * grad_probs, axis=-1, keepdims=True))) * score_scale
    grad_scores = grad_scores.astype(jnp.bfloat16).astype(jnp.float32)
    grad_query = jnp.einsum('bhqk,bkhe->bqhe', grad_scores, keys_f)
    grad_keys = jnp.einsum('bhqk,bqhe->bkhe', grad_scores, query)
    grad_value = jnp.einsum('bhqk,bqhe->bkhe', soft_low.astype(jnp.float32), grad_att_f)
    grad_qkv = jnp.stack([grad_query, grad_keys, grad_value], axis=2).astype(jnp.bfloat16)
    grad_qkv = grad_qkv.reshape(windows, members, 3 * channels)
    normalized_gradient = jnp.dot(grad_qkv.reshape(-1, 3 * channels), w_qkv.T, preferred_element_type=jnp.float32)
    normalized_gradient = normalized_gradient.reshape(windows, members, channels)
    gradient_average = lax.optimization_barrier(jnp.mean(normalized_gradient, axis=-1, keepdims=True))
    projected_average = lax.optimization_barrier(jnp.mean(normalized_gradient * standardized_input, axis=-1, keepdims=True))
    layernorm_gradient = inverse_deviation * (normalized_gradient - gradient_average - standardized_input * projected_average)
    grad_win = (cot_win.astype(jnp.float32) + layernorm_gradient).astype(jnp.bfloat16)
    return (grad_win, normalized_tokens, attended.reshape(windows, members, channels), grad_qkv)

def reference(tokens, cotangent, w_qkv, w_out):
    rows_all, cols_all, channels = tokens.shape

    def to_windows(field):
        shaped = field.reshape(GRID, rows_all // GRID, GRID, cols_all // GRID, channels)
        return shaped.transpose(1, 3, 0, 2, 4).reshape(rows_all // GRID, cols_all // GRID, GRID * GRID, channels)
    token_rows = to_windows(tokens)
    cot_rows = to_windows(cotangent)

    def accumulate(carry, blocks):
        grad_win, normalized_tokens, attended, grad_qkv = window_pass(blocks[0], blocks[1], w_qkv, w_out)
        sum_qkv = carry[0] + jnp.dot(normalized_tokens.reshape(-1, channels).T, grad_qkv.reshape(-1, 3 * channels), preferred_element_type=jnp.float32)
        sum_out = carry[1] + jnp.dot(attended.reshape(-1, channels).T, blocks[1].reshape(-1, channels), preferred_element_type=jnp.float32)
        return ((sum_qkv, sum_out), grad_win)
    zero_sums = (jnp.zeros((channels, 3 * channels), jnp.float32), jnp.zeros((channels, channels), jnp.float32))
    (sum_qkv, sum_out), grads = lax.scan(accumulate, zero_sums, (token_rows, cot_rows))
    grad_tokens = grads.reshape(rows_all // GRID, cols_all // GRID, GRID, GRID, channels)
    grad_tokens = grad_tokens.transpose(2, 0, 3, 1, 4).reshape(rows_all, cols_all, channels)
    factor = float(TOKENS) ** (-0.5)
    return (grad_tokens, sum_qkv * factor, sum_out * factor)
```

```python
import functools

import jax
import jax.numpy as jnp
from jax import lax
from jax.experimental import pallas as pl
from jax.experimental.pallas import tpu as pltpu
from jax.sharding import PartitionSpec as P

MESH = pl.DeviceIdType.MESH
F32 = jnp.float32
BF16 = jnp.bfloat16

D = 512
HEADS = 16
HEAD = 32
EPS = 1e-05
CHIPS = 64
MEMBERS = 64
CHUNKS = 2
NW = 8
ROWS = NW * MEMBERS
STRIDE = 27
SCALE = HEAD ** (-0.5)
LOG2E = 1.4426950408889634
FACTOR = 131072.0 ** (-0.5)


def place():
    gy = lax.axis_index("gy")
    gx = lax.axis_index("gx")
    return gy // 4, (gx // 4) * 2 + (gy // 2) % 2, gx % 4, gy % 2


def device(x, y, z, core):
    return (x * 4 + (y % 2) * 2 + core, (y // 2) * 4 + z)


def shifted(here, k):
    x, y, z, core = here
    s = (k * STRIDE) % CHIPS
    return (x + s // 16) % 4, (y + (s // 4) % 4) % 4, (z + s % 4) % 4, core


def send_to_all(here, source, target, send_sem, recv_sem):
    me = here[0] * 16 + here[1] * 4 + here[2]

    def one(k, carry):
        x, y, z, core = shifted(here, k)
        chip = x * 16 + y * 4 + z
        pltpu.make_async_remote_copy(
            src_ref=source.at[chip],
            dst_ref=target.at[me],
            send_sem=send_sem,
            recv_sem=recv_sem,
            device_id=device(x, y, z, core),
            device_id_type=MESH,
        ).start()
        return carry

    lax.fori_loop(1, CHIPS, one, 0)
    target[me] = source[me]


def wait_all(buffer, sem):
    part = buffer.at[pl.ds(0, CHIPS - 1)]
    pltpu.make_async_copy(part, part, sem).wait()


def dot(a, b):
    return jnp.dot(a, b, preferred_element_type=F32)


def dot_t(a, b):
    return lax.dot_general(a, b, (((1,), (1,)), ((), ())), preferred_element_type=F32)


def dot_0(a, b):
    return lax.dot_general(a, b, (((0,), (0,)), ((), ())), preferred_element_type=F32)


def kernel(
    tok_hbm, cot_hbm, wqkv_hbm, wout_hbm,
    gt_ref, gw_ref, gwo_ref,
    tok, cot, wqkv, wout,
    sent, got, tok_f, cot_f, xhat, rstd, normed, cot_w, qkv, gatt, att, dqkv, gnorm, back_f,
    back, home, dw, dwo, part, other, summed, pieces,
    load_sem, in_send, in_recv, out_send, out_recv, x_send, x_recv, r_send, r_recv,
):
    here = place()
    core = here[3]
    me = here[0] * 16 + here[1] * 4 + here[2]

    loads = [
        pltpu.make_async_copy(tok_hbm, tok, load_sem.at[0]),
        pltpu.make_async_copy(cot_hbm, cot, load_sem.at[1]),
        pltpu.make_async_copy(wqkv_hbm, wqkv, load_sem.at[2]),
        pltpu.make_async_copy(wout_hbm, wout, load_sem.at[3]),
    ]
    for load in loads:
        load.start()

    barrier = pltpu.get_barrier_semaphore()

    def greet(k, carry):
        pl.semaphore_signal(barrier, inc=1, device_id=device(*shifted(here, k)), device_id_type=MESH)
        return carry

    lax.fori_loop(1, CHIPS, greet, 0)
    pl.semaphore_signal(
        barrier, inc=1, device_id=device(here[0], here[1], here[2], 1 - core), device_id_type=MESH
    )
    loads[0].wait()
    loads[1].wait()

    def pack(p, carry):
        cells = (p // 4, pl.ds(pl.multiple_of((p % 4) * 16, 16), 16))
        t = tok[cells].astype(F32)
        c = cot[cells].astype(F32)
        for i in range(CHUNKS):
            rows = slice(i * NW, (i + 1) * NW)
            sent[i, p] = jnp.concatenate([t[rows], c[rows]], axis=0).astype(BF16)
        return carry

    lax.fori_loop(0, CHIPS, pack, 0)
    pl.semaphore_wait(barrier, CHIPS)
    for i in range(CHUNKS):
        send_to_all(here, sent.at[i], got.at[i], in_send.at[i], in_recv.at[i])
    loads[2].wait()
    loads[3].wait()

    lane = lax.broadcasted_iota(jnp.int32, (MEMBERS, 128), 1) // HEAD

    for i in range(CHUNKS):
        wait_all(got.at[i], in_recv.at[i])

        def unpack(p, carry):
            block = got[i, p].astype(F32)
            rows = pl.ds(pl.multiple_of(p * NW, NW), NW)
            for t in range(4):
                lanes = slice(t * 128, (t + 1) * 128)
                tok_f[t, rows, :] = block[:NW, lanes]
                cot_f[t, rows, :] = block[NW:, lanes]
            return carry

        lax.fori_loop(0, CHIPS, unpack, 0)

        for j in range(NW):
            window = pl.ds(j * MEMBERS, MEMBERS)
            strided = pl.ds(j, MEMBERS, stride=NW)
            values = jnp.concatenate([tok_f[t, strided, :] for t in range(4)], axis=1)
            mean = jnp.mean(values, axis=-1, keepdims=True)
            centred = values - mean
            variance = jnp.mean(centred * centred, axis=-1, keepdims=True)
            inverse = lax.rsqrt(variance + EPS)
            standard = centred * inverse
            xhat[window, :] = standard
            rstd[window, :] = jnp.broadcast_to(inverse, (MEMBERS, 128))
            normed[window, :] = standard.astype(BF16)
            cot_w[window, :] = jnp.concatenate(
                [cot_f[t, strided, :] for t in range(4)], axis=1
            ).astype(BF16)

        for n in range(3):
            columns = slice(n * D, (n + 1) * D)
            qkv[:, columns] = dot(normed[...], wqkv[:, columns]).astype(BF16)
        gatt[...] = dot_t(cot_w[...], wout[...]).astype(BF16)

        def attend(w, carry):
            window = pl.ds(pl.multiple_of(w * MEMBERS, MEMBERS), MEMBERS)
            for g in range(4):
                lanes = [slice(n * D + g * 128, n * D + (g + 1) * 128) for n in range(3)]
                q, k, v = (qkv[window, lanes[n]] for n in range(3))
                go = gatt[window, lanes[0]]
                zero = jnp.zeros_like(q)
                qs = jnp.concatenate([jnp.where(lane == h, q, zero) for h in range(4)], axis=0)
                gs = jnp.concatenate([jnp.where(lane == h, go, zero) for h in range(4)], axis=0)
                s = dot_t(k, qs) * (SCALE * LOG2E)
                e = jnp.exp2(s - jnp.max(s, axis=0, keepdims=True))
                p = e * (1.0 / jnp.sum(e, axis=0, keepdims=True))
                gp = dot_t(v, gs)
                ds = p * (gp - jnp.sum(p * gp, axis=0, keepdims=True)) * SCALE
                ds = ds.astype(BF16)
                low = p.astype(BF16)
                dqkv[window, lanes[1]] = dot(ds, qs).astype(BF16)
                dqkv[window, lanes[2]] = dot(low, gs).astype(BF16)
                a4 = dot_0(low, v)
                q4 = dot_0(ds, k)

                def diagonal(blocks):
                    total = blocks[3 * MEMBERS :]
                    for h in range(3):
                        total = jnp.where(
                            lane == h, blocks[h * MEMBERS : (h + 1) * MEMBERS], total
                        )
                    return total.astype(BF16)

                att[window, lanes[0]] = diagonal(a4)
                dqkv[window, lanes[0]] = diagonal(q4)
            return carry

        lax.fori_loop(0, NW, attend, 0)

        for n in range(3):
            columns = slice(n * D, (n + 1) * D)
            term = dot_0(normed[...], dqkv[:, columns])
            dw[:, columns] = term if i == 0 else dw[:, columns] + term
        term = dot_0(att[...], cot_w[...])
        dwo[...] = term if i == 0 else dwo[...] + term

        if i == CHUNKS - 1:

            def regroup(t, carry):
                owner_x, y_lo, owner_core, y_hi, half = t // 16, (t // 8) % 2, (t // 4) % 2, (t // 2) % 2, t % 2
                rows = pl.ds(pl.multiple_of(t * 8, 8), 8)
                blocks = [dw[rows, n * D : (n + 1) * D] for n in range(3)] + [dwo[rows, :]]
                chip = owner_x * 16 + (y_hi * 2 + y_lo) * 4 + half * 2
                part[owner_core, chip] = jnp.concatenate([b[:4] for b in blocks], axis=0).astype(BF16)
                part[owner_core, chip + 1] = jnp.concatenate([b[4:] for b in blocks], axis=0).astype(BF16)
                return carry

            lax.fori_loop(0, D // 8, regroup, 0)
            cross = pltpu.make_async_remote_copy(
                src_ref=part.at[1 - core],
                dst_ref=other,
                send_sem=x_send,
                recv_sem=x_recv,
                device_id=device(here[0], here[1], here[2], 1 - core),
                device_id_type=MESH,
            )
            cross.start()

        gnorm[...] = dot_t(dqkv[...], wqkv[...])
        for j in range(NW):
            window = pl.ds(j * MEMBERS, MEMBERS)
            strided = pl.ds(j, MEMBERS, stride=NW)
            g = gnorm[window, :]
            standard = xhat[window, :]
            average = jnp.mean(g, axis=-1, keepdims=True)
            projected = jnp.mean(g * standard, axis=-1, keepdims=True)
            layer = rstd[window, 0:1] * (g - average - standard * projected)
            result = cot_w[window, :].astype(F32) + layer
            for t in range(4):
                back_f[t, strided, :] = result[:, t * 128 : (t + 1) * 128]

        def repack(p, carry):
            rows = pl.ds(pl.multiple_of(p * NW, NW), NW)
            left = jnp.concatenate([back_f[t, rows, :] for t in range(2)], axis=1)
            right = jnp.concatenate([back_f[t, rows, :] for t in range(2, 4)], axis=1)
            back[i, p] = jnp.concatenate([left, right], axis=0).astype(BF16)
            return carry

        lax.fori_loop(0, CHIPS, repack, 0)
        send_to_all(here, back.at[i], home.at[i], out_send.at[i], out_recv.at[i])

    cross.wait_recv()

    def pair(p, carry):
        summed[p] = (part[core, p].astype(F32) + other[p].astype(F32)).astype(BF16)
        return carry

    lax.fori_loop(0, CHIPS, pair, 0)
    send_to_all(here, summed, pieces, r_send, r_recv)

    for i in range(CHUNKS):
        wait_all(home.at[i], out_recv.at[i])

    def unfold(p, carry):
        halves = []
        for i in range(CHUNKS):
            block = home[i, p].astype(F32)
            halves.append(jnp.concatenate([block[:NW], block[NW:]], axis=1))
        cells = (p // 4, pl.ds(pl.multiple_of((p % 4) * 16, 16), 16))
        gt_ref[cells] = jnp.concatenate(halves, axis=0).astype(BF16)
        return carry

    lax.fori_loop(0, CHIPS, unfold, 0)

    wait_all(pieces, r_recv)
    total = lax.fori_loop(
        0, CHIPS, lambda p, acc: acc + pieces[p].astype(F32), jnp.zeros((16, D), F32)
    )
    total = total * FACTOR
    for n in range(3):
        gw_ref[:, n * D : (n + 1) * D] = total[n * 4 : (n + 1) * 4]
    gwo_ref[...] = total[12:]

    cross.wait_send()
    for i in range(CHUNKS):
        wait_all(sent.at[i], in_send.at[i])
        wait_all(back.at[i], out_send.at[i])
    wait_all(summed, r_send)


def body(tokens, cotangent, w_qkv, w_out):
    rows, columns, _ = tokens.shape
    vmem = pltpu.VMEM
    dma = pltpu.SemaphoreType.DMA
    return pl.pallas_call(
        kernel,
        out_shape=(
            jax.ShapeDtypeStruct((rows, columns, D), BF16),
            jax.ShapeDtypeStruct((4, 3 * D), F32),
            jax.ShapeDtypeStruct((4, D), F32),
        ),
        in_specs=[pl.BlockSpec(memory_space=pl.ANY)] * 4,
        out_specs=[pl.BlockSpec(memory_space=vmem)] * 3,
        scratch_shapes=[
            vmem((rows, columns, D), BF16),
            vmem((rows, columns, D), BF16),
            vmem((D, 3 * D), BF16),
            vmem((D, D), BF16),
            vmem((CHUNKS, CHIPS, 2 * NW, D), BF16),
            vmem((CHUNKS, CHIPS, 2 * NW, D), BF16),
            vmem((4, ROWS, 128), F32),
            vmem((4, ROWS, 128), F32),
            vmem((ROWS, D), F32),
            vmem((ROWS, 128), F32),
            vmem((ROWS, D), BF16),
            vmem((ROWS, D), BF16),
            vmem((ROWS, 3 * D), BF16),
            vmem((ROWS, D), BF16),
            vmem((ROWS, D), BF16),
            vmem((ROWS, 3 * D), BF16),
            vmem((ROWS, D), F32),
            vmem((4, ROWS, 128), F32),
            vmem((CHUNKS, CHIPS, 16, NW * D // 16), BF16),
            vmem((CHUNKS, CHIPS, 16, NW * D // 16), BF16),
            vmem((D, 3 * D), F32),
            vmem((D, D), F32),
            vmem((2, CHIPS, 16, D), BF16),
            vmem((CHIPS, 16, D), BF16),
            vmem((CHIPS, 16, D), BF16),
            vmem((CHIPS, 16, D), BF16),
            dma((4,)),
            dma((CHUNKS,)), dma((CHUNKS,)),
            dma((CHUNKS,)), dma((CHUNKS,)),
            dma(()), dma(()),
            dma(()), dma(()),
        ],
        compiler_params=pltpu.CompilerParams(
            collective_id=0, has_side_effects=True, vmem_limit_bytes=60 << 20
        ),
        name="grid_attention_backward",
    )(tokens, cotangent, w_qkv, w_out)


def solution(mesh):
    in_specs = (P("gy", "gx", None), P("gy", "gx", None), P(), P())
    out_specs = (P("gy", "gx", None), P(("gy", "gx"), None), P(("gy", "gx"), None))
    return jax.shard_map(body, mesh=mesh, in_specs=in_specs, out_specs=out_specs, check_vma=False)
```

```python
import jax
import jax.numpy as jnp
from jax import lax
from jax.experimental import pallas as pl
from jax.experimental.pallas import tpu as pltpu
from jax.sharding import PartitionSpec as P

MESH = pl.DeviceIdType.MESH
F32 = jnp.float32
BF16 = jnp.bfloat16

D = 512
HEAD = 32
EPS = 1e-05
CHIPS = 64
MEMBERS = 64
WINDOWS = 16
CHUNKS = 2
NW = WINDOWS // CHUNKS
ROWS = NW * MEMBERS
KEEP = CHUNKS // 2
IN_LANES = 2 * NW * D // 16
OUT_LANES = NW * D // 16
TOGETHER = 2
SCALE = HEAD ** (-0.5)
LOG2E = 1.4426950408889634
FACTOR = 131072.0 ** (-0.5)


def place():
    gy = lax.axis_index("gy")
    gx = lax.axis_index("gx")
    return gy // 4, (gx // 4) * 2 + (gy // 2) % 2, gx % 4, gy % 2


def device(x, y, z, core):
    return (x * 4 + (y % 2) * 2 + core, (y // 2) * 4 + z)


def chip_of(x, y, z):
    return x * 16 + y * 4 + z


def moved(here, x, y, z):
    return (here[0] + x) % 4, (here[1] + y) % 4, (here[2] + z) % 4, here[3]


def for_line(here, act):
    def step(d, carry):
        act(moved(here, d, 0, 0))
        act(moved(here, 0, d, 0))
        act(moved(here, 0, 0, d))
        return carry

    lax.fori_loop(1, 4, step, 0)


def for_plane(here, act):
    def step(k, carry):
        a, b = k // 3 + 1, k % 3 + 1
        act(moved(here, a, b, 0))
        act(moved(here, 0, a, b))
        act(moved(here, b, 0, a))
        return carry

    lax.fori_loop(0, 9, step, 0)


def for_space(here, act):
    def step(k, carry):
        s = (k * 10) % 27
        act(moved(here, s // 9 + 1, (s // 3) % 3 + 1, s % 3 + 1))
        return carry

    lax.fori_loop(0, 27, step, 0)


def for_all(here, act):
    def step(k, carry):
        s = (k * 27) % CHIPS
        act(moved(here, s // 16, (s // 4) % 4, s % 4))
        return carry

    lax.fori_loop(1, CHIPS, step, 0)


def sender(here, source, target, send_sem, recv_sem):
    me = chip_of(*here[:3])

    def act(there):
        pltpu.make_async_remote_copy(
            src_ref=source.at[chip_of(*there[:3])],
            dst_ref=target.at[me],
            send_sem=send_sem,
            recv_sem=recv_sem,
            device_id=device(*there),
            device_id_type=MESH,
        ).start()

    return act


def wait_all(buffer, sem):
    part = buffer.at[pl.ds(0, CHIPS - 1)]
    pltpu.make_async_copy(part, part, sem).wait()


def dot(a, b):
    return jnp.dot(a, b, preferred_element_type=F32)


def dot_t(a, b):
    return lax.dot_general(a, b, (((1,), (1,)), ((), ())), preferred_element_type=F32)


def dot_0(a, b):
    return lax.dot_general(a, b, (((0,), (0,)), ((), ())), preferred_element_type=F32)


def fold(rows):
    n, width = rows.shape
    parts = 16 // n
    lanes = width // parts
    return jnp.concatenate([rows[:, i * lanes : (i + 1) * lanes] for i in range(parts)], axis=0)


def unfold(block, n):
    parts = 16 // n
    return jnp.concatenate([block[i * n : (i + 1) * n] for i in range(parts)], axis=1)


def attend(w, base, qkv, gatt, dqkv, att):
    lane = lax.broadcasted_iota(jnp.int32, (MEMBERS, 128), 1) // HEAD
    zero = jnp.zeros((MEMBERS, 128), BF16)

    def spread(a):
        return jnp.concatenate([jnp.where(lane == h, a, zero) for h in range(4)], axis=0)

    def diagonal(blocks):
        total = blocks[3 * MEMBERS :]
        for h in range(3):
            total = jnp.where(lane == h, blocks[h * MEMBERS : (h + 1) * MEMBERS], total)
        return total.astype(BF16)

    units = []
    for i in range(TOGETHER):
        start = (w * TOGETHER + i) * MEMBERS
        inside = pl.ds(pl.multiple_of(start, MEMBERS), MEMBERS)
        kept = pl.ds(pl.multiple_of(base + start, MEMBERS), MEMBERS)
        for g in range(4):
            units.append((inside, kept, [slice(n * D + g * 128, n * D + (g + 1) * 128) for n in range(3)]))
    qs = [spread(qkv[r, c[0]]) for r, _, c in units]
    gs = [spread(gatt[r, c[0]]) for r, _, c in units]
    s = [dot_t(qkv[r, c[1]], b) * (SCALE * LOG2E) for (r, _, c), b in zip(units, qs)]
    gp = [dot_t(qkv[r, c[2]], b) for (r, _, c), b in zip(units, gs)]
    e = [jnp.exp2(a - jnp.max(a, axis=0, keepdims=True)) for a in s]
    p = [a * (1.0 / jnp.sum(a, axis=0, keepdims=True)) for a in e]
    low = [a.astype(BF16) for a in p]
    ds = [
        (a * (b - jnp.sum(a * b, axis=0, keepdims=True)) * SCALE).astype(BF16)
        for a, b in zip(p, gp)
    ]
    for n, (r, kept, c) in enumerate(units):
        dqkv[kept, c[1]] = dot(ds[n], qs[n]).astype(BF16)
        dqkv[kept, c[2]] = dot(low[n], gs[n]).astype(BF16)
    for n, (r, kept, c) in enumerate(units):
        att[kept, c[0]] = diagonal(dot_0(low[n], qkv[r, c[2]]))
        dqkv[kept, c[0]] = diagonal(dot_0(ds[n], qkv[r, c[1]]))


def kernel(
    tok_hbm, cot_hbm, wqkv_hbm, wout_hbm,
    home, total_ref,
    tok, cot, wqkv, wout,
    sent, got, both_f, xhat, rstd, normed, cot_w, qkv, gatt, att, dqkv, gnorm, back_f,
    back, dw, dwo, part, other, summed, pieces,
    load_sem, line_sem, space_sem, own_sem,
    in_send, in_recv, out_send, out_recv, x_send, x_recv, r_send, r_recv,
):
    here = place()
    core = here[3]
    me = chip_of(*here[:3])
    partner = device(here[0], here[1], here[2], 1 - core)

    loads = [
        pltpu.make_async_copy(tok_hbm, tok, load_sem.at[0]),
        pltpu.make_async_copy(cot_hbm, cot, load_sem.at[1]),
        pltpu.make_async_copy(wqkv_hbm, wqkv, load_sem.at[2]),
        pltpu.make_async_copy(wout_hbm, wout, load_sem.at[3]),
    ]
    for load in loads:
        load.start()

    barrier = pltpu.get_barrier_semaphore()

    def signal(sem):
        return lambda there: pl.semaphore_signal(
            sem, inc=1, device_id=device(*there), device_id_type=MESH
        )

    for_line(here, signal(barrier))
    pl.semaphore_signal(barrier, inc=1, device_id=partner, device_id_type=MESH)
    loads[0].wait()
    loads[1].wait()

    def pack(p, carry):
        cells = (p // 4, pl.ds(pl.multiple_of((p % 4) * 16, 16), 16))
        t = tok[cells].astype(F32)
        c = cot[cells].astype(F32)
        for i in range(CHUNKS):
            rows = slice(i * NW, (i + 1) * NW)
            sent[i, p] = fold(jnp.concatenate([t[rows], c[rows]], axis=0)).astype(BF16)
        return carry

    lax.fori_loop(0, CHIPS, pack, 0, unroll=2)
    for i in range(CHUNKS):
        got[i, me] = sent[i, me]

    first = sender(here, sent.at[0], got.at[0], in_send.at[0], in_recv.at[0])
    pl.semaphore_wait(barrier, 10)
    for_line(here, signal(line_sem))
    for_line(here, first)
    pl.semaphore_wait(line_sem, 9)
    for d in range(1, 4):
        signal(space_sem)(moved(here, d, 0, 0))
    for_plane(here, first)
    pl.semaphore_wait(space_sem, 3)
    for_space(here, first)

    def send_in(i):
        for_all(here, sender(here, sent.at[i], got.at[i], in_send.at[i], in_recv.at[i]))

    send_in(1)
    loads[2].wait()
    loads[3].wait()

    for i in range(CHUNKS):
        wait_all(got.at[i], in_recv.at[i])
        if i + 2 < CHUNKS:
            send_in(i + 2)
        base = (i % KEEP) * ROWS
        kept = slice(base, base + ROWS)

        def unpack(p, carry):
            block = unfold(got[i, p].astype(F32), 2 * NW) if NW < 8 else got[i, p].astype(F32)
            rows = pl.ds(pl.multiple_of(p * 2 * NW, 8), 2 * NW)
            for t in range(4):
                both_f[t, rows, :] = block[:, t * 128 : (t + 1) * 128]
            return carry

        lax.fori_loop(0, CHIPS, unpack, 0, unroll=4)

        for j in range(NW):
            window = slice(j * MEMBERS, (j + 1) * MEMBERS)
            members = pl.ds(j, MEMBERS, stride=2 * NW)
            values = jnp.concatenate([both_f[t, members, :] for t in range(4)], axis=1)
            mean = jnp.mean(values, axis=-1, keepdims=True)
            centred = values - mean
            variance = jnp.mean(centred * centred, axis=-1, keepdims=True)
            inverse = lax.rsqrt(variance + EPS)
            standard = centred * inverse
            xhat[window, :] = standard
            rstd[window, :] = jnp.broadcast_to(inverse, (MEMBERS, 128))
            low = slice(base + j * MEMBERS, base + (j + 1) * MEMBERS)
            normed[low, :] = standard.astype(BF16)
            members = pl.ds(NW + j, MEMBERS, stride=2 * NW)
            cot_w[low, :] = jnp.concatenate(
                [both_f[t, members, :] for t in range(4)], axis=1
            ).astype(BF16)

        for n in range(3):
            columns = slice(n * D, (n + 1) * D)
            qkv[:, columns] = dot(normed[kept, :], wqkv[:, columns]).astype(BF16)
        gatt[...] = dot_t(cot_w[kept, :], wout[...]).astype(BF16)

        def attention(w, carry):
            attend(w, base, qkv, gatt, dqkv, att)
            return carry

        lax.fori_loop(0, NW // TOGETHER, attention, 0)

        if i % KEEP == KEEP - 1:
            for n in range(3):
                columns = slice(n * D, (n + 1) * D)
                term = dot_0(normed[...], dqkv[:, columns])
                dw[:, columns] = term if i < KEEP else dw[:, columns] + term
            term = dot_0(att[...], cot_w[...])
            dwo[...] = term if i < KEEP else dwo[...] + term

        if i == CHUNKS - 1:

            def regroup(owner_core):
                def step(t, carry):
                    x, y_lo, y_hi, half = t // 8, (t // 4) % 2, (t // 2) % 2, t % 2
                    tile = x * 16 + y_lo * 8 + owner_core * 4 + y_hi * 2 + half
                    rows = pl.ds(pl.multiple_of(tile * 8, 8), 8)
                    blocks = [dw[rows, n * D : (n + 1) * D] for n in range(3)] + [dwo[rows, :]]
                    chip = chip_of(x, y_hi * 2 + y_lo, half * 2)
                    for k in range(2):
                        piece = [b[k * 4 : (k + 1) * 4] for b in blocks]
                        part[owner_core, chip + k] = jnp.concatenate(piece, axis=0).astype(BF16)
                    return carry

                lax.fori_loop(0, CHIPS // 2, step, 0, unroll=2)

            regroup(1 - core)
            cross = pltpu.make_async_remote_copy(
                src_ref=part.at[1 - core],
                dst_ref=other,
                send_sem=x_send,
                recv_sem=x_recv,
                device_id=partner,
                device_id_type=MESH,
            )
            cross.start()
            regroup(core)

        gnorm[...] = dot_t(dqkv[kept, :], wqkv[...])
        for j in range(NW):
            window = slice(j * MEMBERS, (j + 1) * MEMBERS)
            members = pl.ds(j, MEMBERS, stride=NW)
            g = gnorm[window, :]
            standard = xhat[window, :]
            average = jnp.mean(g, axis=-1, keepdims=True)
            projected = jnp.mean(g * standard, axis=-1, keepdims=True)
            layer = rstd[window, 0:1] * (g - average - standard * projected)
            result = cot_w[base + j * MEMBERS : base + (j + 1) * MEMBERS, :].astype(F32) + layer
            for t in range(4):
                back_f[t, members, :] = result[:, t * 128 : (t + 1) * 128]

        def repack(b, carry):
            rows = pl.ds(pl.multiple_of(b * 8, 8), 8)
            block = jnp.concatenate([back_f[t, rows, :] for t in range(4)], axis=1)
            for k in range(8 // NW):
                back[i, b * (8 // NW) + k] = fold(block[k * NW : (k + 1) * NW]).astype(BF16)
            return carry

        lax.fori_loop(0, ROWS // 8, repack, 0, unroll=2)
        for_all(here, sender(here, back.at[i], home.at[i], out_send.at[i], out_recv.at[i]))
        pltpu.make_async_copy(back.at[i, me], home.at[i, me], own_sem.at[i]).start()

    cross.wait_recv()

    def pair(b, carry):
        for k in range(4):
            p = b * 4 + k
            summed[p] = (part[core, p].astype(F32) + other[p].astype(F32)).astype(BF16)
        return carry

    lax.fori_loop(0, CHIPS // 4, pair, 0)
    for_all(here, sender(here, summed, pieces, r_send, r_recv))
    pieces[me] = summed[me]

    for i in range(CHUNKS):
        wait_all(home.at[i], out_recv.at[i])
        pltpu.make_async_copy(back.at[i, me], home.at[i, me], own_sem.at[i]).wait()
    wait_all(pieces, r_recv)

    def add(b, acc):
        for k in range(4):
            acc = acc + pieces[b * 4 + k].astype(F32)
        return acc

    total_ref[...] = lax.fori_loop(0, CHIPS // 4, add, jnp.zeros((16, D), F32))

    cross.wait_send()
    for i in range(CHUNKS):
        wait_all(sent.at[i], in_send.at[i])
        wait_all(back.at[i], out_send.at[i])
    wait_all(summed, r_send)


def finish(home, total, gt, gw, gwo):
    def cells(b, carry):
        p = pl.ds(b, 1)
        blocks = [home[i, p][0].astype(F32) for i in range(CHUNKS)]
        value = jnp.concatenate([unfold(block, NW) for block in blocks], axis=0)
        gt[b // 4, pl.ds(pl.multiple_of((b % 4) * 16, 16), 16)] = value.astype(BF16)
        return carry

    lax.fori_loop(0, 16, cells, 0, unroll=4)

    @pl.when(pl.program_id(0) == 0)
    def _():
        scaled = total[...] * FACTOR
        for n in range(3):
            gw[:, n * D : (n + 1) * D] = scaled[n * 4 : (n + 1) * 4]
        gwo[...] = scaled[12:]


def body(tokens, cotangent, w_qkv, w_out):
    rows, columns, _ = tokens.shape
    vmem = pltpu.VMEM
    dma = pltpu.SemaphoreType.DMA
    regular = pltpu.SemaphoreType.REGULAR
    home, total = pl.pallas_call(
        kernel,
        out_shape=(
            jax.ShapeDtypeStruct((CHUNKS, CHIPS, 16, OUT_LANES), BF16),
            jax.ShapeDtypeStruct((16, D), F32),
        ),
        in_specs=[pl.BlockSpec(memory_space=pl.ANY)] * 4,
        out_specs=[pl.BlockSpec(memory_space=pl.ANY), pl.BlockSpec(memory_space=vmem)],
        scratch_shapes=[
            vmem((rows, columns, D), BF16),
            vmem((rows, columns, D), BF16),
            vmem((D, 3 * D), BF16),
            vmem((D, D), BF16),
            vmem((CHUNKS, CHIPS, 16, IN_LANES), BF16),
            vmem((CHUNKS, CHIPS, 16, IN_LANES), BF16),
            vmem((4, 2 * ROWS, 128), F32),
            vmem((ROWS, D), F32),
            vmem((ROWS, 128), F32),
            vmem((KEEP * ROWS, D), BF16),
            vmem((KEEP * ROWS, D), BF16),
            vmem((ROWS, 3 * D), BF16),
            vmem((ROWS, D), BF16),
            vmem((KEEP * ROWS, D), BF16),
            vmem((KEEP * ROWS, 3 * D), BF16),
            vmem((ROWS, D), F32),
            vmem((4, ROWS, 128), F32),
            vmem((CHUNKS, CHIPS, 16, OUT_LANES), BF16),
            vmem((D, 3 * D), F32),
            vmem((D, D), F32),
            vmem((2, CHIPS, 16, D), BF16),
            vmem((CHIPS, 16, D), BF16),
            vmem((CHIPS, 16, D), BF16),
            vmem((CHIPS, 16, D), BF16),
            dma((4,)), regular, regular, dma((CHUNKS,)),
            dma((CHUNKS,)), dma((CHUNKS,)),
            dma((CHUNKS,)), dma((CHUNKS,)),
            dma(()), dma(()),
            dma(()), dma(()),
        ],
        compiler_params=pltpu.CompilerParams(
            collective_id=0, has_side_effects=True, vmem_limit_bytes=60 << 20
        ),
        name="grid_attention_backward",
    )(tokens, cotangent, w_qkv, w_out)
    steps = 4
    return pl.pallas_call(
        finish,
        grid=(steps,),
        out_shape=(
            jax.ShapeDtypeStruct((rows, columns, D), BF16),
            jax.ShapeDtypeStruct((4, 3 * D), F32),
            jax.ShapeDtypeStruct((4, D), F32),
        ),
        in_specs=[
            pl.BlockSpec((CHUNKS, CHIPS // steps, 16, OUT_LANES), lambda s: (0, s, 0, 0)),
            pl.BlockSpec((16, D), lambda s: (0, 0)),
        ],
        out_specs=[
            pl.BlockSpec((rows // steps, columns, D), lambda s: (s, 0, 0)),
            pl.BlockSpec((4, 3 * D), lambda s: (0, 0)),
            pl.BlockSpec((4, D), lambda s: (0, 0)),
        ],
        compiler_params=pltpu.CompilerParams(vmem_limit_bytes=60 << 20),
        name="cells_from_blocks",
    )(home, total)


def solution(mesh):
    in_specs = (P("gy", "gx", None), P("gy", "gx", None), P(), P())
    out_specs = (P("gy", "gx", None), P(("gy", "gx"), None), P(("gy", "gx"), None))
    return jax.shard_map(body, mesh=mesh, in_specs=in_specs, out_specs=out_specs, check_vma=False)
```

```python
import jax
import jax.numpy as jnp
from jax import lax
from jax.experimental import pallas as pl
from jax.experimental.pallas import tpu as pltpu
from jax.sharding import PartitionSpec as P

MESH = pl.DeviceIdType.MESH
F32 = jnp.float32
BF16 = jnp.bfloat16

D = 512
HEAD = 32
EPS = 1e-05
CHIPS = 64
MEMBERS = 64
WINDOWS = 16
CHUNKS = 2
NW = WINDOWS // CHUNKS
ROWS = NW * MEMBERS
KEEP = CHUNKS // 2
IN_LANES = 2 * NW * D // 16
OUT_LANES = NW * D // 16
TOGETHER = 4
SCALE = HEAD ** (-0.5)
LOG2E = 1.4426950408889634
FACTOR = 131072.0 ** (-0.5)


def place():
    gy = lax.axis_index("gy")
    gx = lax.axis_index("gx")
    return gy // 4, (gx // 4) * 2 + (gy // 2) % 2, gx % 4, gy % 2


def device(x, y, z, core):
    return (x * 4 + (y % 2) * 2 + core, (y // 2) * 4 + z)


def chip_of(x, y, z):
    return x * 16 + y * 4 + z


def moved(here, x, y, z):
    return (here[0] + x) % 4, (here[1] + y) % 4, (here[2] + z) % 4, here[3]


def for_line(here, act):
    def step(d, carry):
        act(moved(here, d, 0, 0))
        act(moved(here, 0, d, 0))
        act(moved(here, 0, 0, d))
        return carry

    lax.fori_loop(1, 4, step, 0)


def for_plane(here, act):
    def step(k, carry):
        a, b = k // 3 + 1, k % 3 + 1
        act(moved(here, a, b, 0))
        act(moved(here, 0, a, b))
        act(moved(here, b, 0, a))
        return carry

    lax.fori_loop(0, 9, step, 0)


def for_space(here, act):
    def step(k, carry):
        s = (k * 10) % 27
        act(moved(here, s // 9 + 1, (s // 3) % 3 + 1, s % 3 + 1))
        return carry

    lax.fori_loop(0, 27, step, 0)


def for_all(here, act):
    def step(k, carry):
        s = (k * 27) % CHIPS
        act(moved(here, s // 16, (s // 4) % 4, s % 4))
        return carry

    lax.fori_loop(1, CHIPS, step, 0)


def sender(here, source, target, send_sem, recv_sem):
    me = chip_of(*here[:3])

    def act(there):
        pltpu.make_async_remote_copy(
            src_ref=source.at[chip_of(*there[:3])],
            dst_ref=target.at[me],
            send_sem=send_sem,
            recv_sem=recv_sem,
            device_id=device(*there),
            device_id_type=MESH,
        ).start()

    return act


def wait_all(buffer, sem):
    part = buffer.at[pl.ds(0, CHIPS - 1)]
    pltpu.make_async_copy(part, part, sem).wait()


def dot(a, b):
    return jnp.dot(a, b, preferred_element_type=F32)


def dot_t(a, b):
    return lax.dot_general(a, b, (((1,), (1,)), ((), ())), preferred_element_type=F32)


def dot_0(a, b):
    return lax.dot_general(a, b, (((0,), (0,)), ((), ())), preferred_element_type=F32)


def fold(rows):
    n, width = rows.shape
    parts = 16 // n
    lanes = width // parts
    return jnp.concatenate([rows[:, i * lanes : (i + 1) * lanes] for i in range(parts)], axis=0)


def unfold(block, n):
    parts = 16 // n
    return jnp.concatenate([block[i * n : (i + 1) * n] for i in range(parts)], axis=1)


def attend(w, base, qkv, gatt, dqkv, att):
    lane = lax.broadcasted_iota(jnp.int32, (MEMBERS, 128), 1) // HEAD
    zero = jnp.zeros((MEMBERS, 128), BF16)

    def spread(a):
        return jnp.concatenate([jnp.where(lane == h, a, zero) for h in range(4)], axis=0)

    def diagonal(blocks):
        total = blocks[3 * MEMBERS :]
        for h in range(3):
            total = jnp.where(lane == h, blocks[h * MEMBERS : (h + 1) * MEMBERS], total)
        return total.astype(BF16)

    units = []
    for i in range(TOGETHER):
        start = (w * TOGETHER + i) * MEMBERS
        inside = pl.ds(pl.multiple_of(start, MEMBERS), MEMBERS)
        kept = pl.ds(pl.multiple_of(base + start, MEMBERS), MEMBERS)
        for g in range(4):
            units.append((inside, kept, [slice(n * D + g * 128, n * D + (g + 1) * 128) for n in range(3)]))
    qs = [spread(qkv[r, c[0]]) for r, _, c in units]
    gs = [spread(gatt[r, c[0]]) for r, _, c in units]
    s = [dot_t(qkv[r, c[1]], b) * (SCALE * LOG2E) for (r, _, c), b in zip(units, qs)]
    gp = [dot_t(qkv[r, c[2]], b) for (r, _, c), b in zip(units, gs)]
    e = [jnp.exp2(a - jnp.max(a, axis=0, keepdims=True)) for a in s]
    p = [a * (1.0 / jnp.sum(a, axis=0, keepdims=True)) for a in e]
    low = [a.astype(BF16) for a in p]
    ds = [
        (a * (b - jnp.sum(a * b, axis=0, keepdims=True)) * SCALE).astype(BF16)
        for a, b in zip(p, gp)
    ]
    for n, (r, kept, c) in enumerate(units):
        dqkv[kept, c[1]] = dot(ds[n], qs[n]).astype(BF16)
        dqkv[kept, c[2]] = dot(low[n], gs[n]).astype(BF16)
    for n, (r, kept, c) in enumerate(units):
        att[kept, c[0]] = diagonal(dot_0(low[n], qkv[r, c[2]]))
        dqkv[kept, c[0]] = diagonal(dot_0(ds[n], qkv[r, c[1]]))


def kernel(
    tok_hbm, cot_hbm, wqkv_hbm, wout_hbm,
    home, total_ref,
    tok, cot, wqkv, wout,
    sent, got, both_f, xhat, rstd, normed, cot_w, qkv, gatt, att, dqkv, gnorm, back_f,
    back, dw, dwo, given, taken,
    left, right, left_in, right_in, left_sum, right_sum, left_all, right_all,
    load_sem, line_sem, space_sem, own_sem,
    in_send, in_recv, out_send, out_recv, x_send, x_recv, a_send, a_recv, b_send, b_recv,
):
    here = place()
    core = here[3]
    me = chip_of(*here[:3])
    partner = device(here[0], here[1], here[2], 1 - core)

    loads = [
        pltpu.make_async_copy(tok_hbm, tok, load_sem.at[0]),
        pltpu.make_async_copy(cot_hbm, cot, load_sem.at[1]),
        pltpu.make_async_copy(wqkv_hbm, wqkv, load_sem.at[2]),
        pltpu.make_async_copy(wout_hbm, wout, load_sem.at[3]),
    ]
    for load in loads:
        load.start()

    barrier = pltpu.get_barrier_semaphore()

    def signal(sem):
        return lambda there: pl.semaphore_signal(
            sem, inc=1, device_id=device(*there), device_id_type=MESH
        )

    for_line(here, signal(barrier))
    pl.semaphore_signal(barrier, inc=1, device_id=partner, device_id_type=MESH)
    loads[0].wait()
    loads[1].wait()

    def pack(p, carry):
        cells = (p // 4, pl.ds(pl.multiple_of((p % 4) * 16, 16), 16))
        t = tok[cells].astype(F32)
        c = cot[cells].astype(F32)
        for i in range(CHUNKS):
            rows = slice(i * NW, (i + 1) * NW)
            sent[i, p] = fold(jnp.concatenate([t[rows], c[rows]], axis=0)).astype(BF16)
        return carry

    lax.fori_loop(0, CHIPS, pack, 0, unroll=2)
    for i in range(CHUNKS):
        got[i, me] = sent[i, me]

    first = sender(here, sent.at[0], got.at[0], in_send.at[0], in_recv.at[0])
    pl.semaphore_wait(barrier, 10)
    for_line(here, signal(line_sem))
    for_line(here, first)
    pl.semaphore_wait(line_sem, 9)
    for d in range(1, 4):
        signal(space_sem)(moved(here, d, 0, 0))
    for_plane(here, first)
    pl.semaphore_wait(space_sem, 3)
    for_space(here, first)

    def send_in(i):
        for_all(here, sender(here, sent.at[i], got.at[i], in_send.at[i], in_recv.at[i]))

    send_in(1)
    loads[2].wait()
    loads[3].wait()

    for i in range(CHUNKS):
        wait_all(got.at[i], in_recv.at[i])
        if i + 2 < CHUNKS:
            send_in(i + 2)
        base = (i % KEEP) * ROWS
        kept = slice(base, base + ROWS)

        def unpack(p, carry):
            block = unfold(got[i, p].astype(F32), 2 * NW) if NW < 8 else got[i, p].astype(F32)
            rows = pl.ds(pl.multiple_of(p * 2 * NW, 8), 2 * NW)
            for t in range(4):
                both_f[t, rows, :] = block[:, t * 128 : (t + 1) * 128]
            return carry

        lax.fori_loop(0, CHIPS, unpack, 0, unroll=4)

        for j in range(NW):
            window = slice(j * MEMBERS, (j + 1) * MEMBERS)
            members = pl.ds(j, MEMBERS, stride=2 * NW)
            values = jnp.concatenate([both_f[t, members, :] for t in range(4)], axis=1)
            mean = jnp.mean(values, axis=-1, keepdims=True)
            centred = values - mean
            variance = jnp.mean(centred * centred, axis=-1, keepdims=True)
            inverse = lax.rsqrt(variance + EPS)
            standard = centred * inverse
            xhat[window, :] = standard
            rstd[window, :] = jnp.broadcast_to(inverse, (MEMBERS, 128))
            low = slice(base + j * MEMBERS, base + (j + 1) * MEMBERS)
            normed[low, :] = standard.astype(BF16)
            members = pl.ds(NW + j, MEMBERS, stride=2 * NW)
            cot_w[low, :] = jnp.concatenate(
                [both_f[t, members, :] for t in range(4)], axis=1
            ).astype(BF16)

        for n in range(3):
            columns = slice(n * D, (n + 1) * D)
            qkv[:, columns] = dot(normed[kept, :], wqkv[:, columns]).astype(BF16)
        gatt[...] = dot_t(cot_w[kept, :], wout[...]).astype(BF16)

        def attention(w, carry):
            attend(w, base, qkv, gatt, dqkv, att)
            return carry

        lax.fori_loop(0, NW // TOGETHER, attention, 0)

        if i % KEEP == KEEP - 1:
            for n in range(3):
                columns = slice(n * D, (n + 1) * D)
                term = dot_0(normed[...], dqkv[:, columns])
                dw[:, columns] = term if i < KEEP else dw[:, columns] + term
            term = dot_0(att[...], cot_w[...])
            dwo[...] = term if i < KEEP else dwo[...] + term

        if i == CHUNKS - 1:

            def lower(b, carry):
                rows = pl.ds(pl.multiple_of(b * 64 + (1 - core) * 32, 32), 32)
                given[b, :, : 3 * D] = dw[rows, :].astype(BF16)
                given[b, :, 3 * D :] = dwo[rows, :].astype(BF16)
                return carry

            lax.fori_loop(0, 8, lower, 0)
            cross = pltpu.make_async_remote_copy(
                src_ref=given,
                dst_ref=taken,
                send_sem=x_send,
                recv_sem=x_recv,
                device_id=partner,
                device_id_type=MESH,
            )
            cross.start()

        gnorm[...] = dot_t(dqkv[kept, :], wqkv[...])
        for j in range(NW):
            window = slice(j * MEMBERS, (j + 1) * MEMBERS)
            members = pl.ds(j, MEMBERS, stride=NW)
            g = gnorm[window, :]
            standard = xhat[window, :]
            average = jnp.mean(g, axis=-1, keepdims=True)
            projected = jnp.mean(g * standard, axis=-1, keepdims=True)
            layer = rstd[window, 0:1] * (g - average - standard * projected)
            result = cot_w[base + j * MEMBERS : base + (j + 1) * MEMBERS, :].astype(F32) + layer
            for t in range(4):
                back_f[t, members, :] = result[:, t * 128 : (t + 1) * 128]

        def repack(b, carry):
            rows = pl.ds(pl.multiple_of(b * 8, 8), 8)
            block = jnp.concatenate([back_f[t, rows, :] for t in range(4)], axis=1)
            for k in range(8 // NW):
                back[i, b * (8 // NW) + k] = fold(block[k * NW : (k + 1) * NW]).astype(BF16)
            return carry

        lax.fori_loop(0, ROWS // 8, repack, 0, unroll=2)
        for_all(here, sender(here, back.at[i], home.at[i], out_send.at[i], out_recv.at[i]))
        pltpu.make_async_copy(back.at[i, me], home.at[i, me], own_sem.at[i]).start()

    cross.wait_recv()

    def halves(owner_x):
        def step(b, carry):
            y_lo, y_hi = b // 2, b % 2
            block = owner_x * 2 + y_lo
            rows = pl.ds(pl.multiple_of(block * 64 + core * 32 + y_hi * 16, 16), 16)
            theirs = taken[block, pl.ds(pl.multiple_of(y_hi * 16, 16), 16), :].astype(F32)
            mine = jnp.concatenate([dw[rows, :], dwo[rows, :]], axis=1) + theirs
            y = y_hi * 2 + y_lo
            for z in range(4):
                piece = jnp.concatenate(
                    [mine[z * 4 : (z + 1) * 4, n * D : (n + 1) * D] for n in range(4)], axis=0
                ).astype(BF16)
                left[owner_x * 16 + y * 4 + z] = piece[:, : D // 2]
                right[y * 16 + owner_x * 4 + z] = piece[:, D // 2 :]
            return carry

        lax.fori_loop(0, 4, step, 0)

    def quarter(source, target, k, sem, there):
        return pltpu.make_async_remote_copy(
            src_ref=source.at[pl.ds(pl.multiple_of(k * 16, 16), 16)],
            dst_ref=target,
            send_sem=a_send.at[sem],
            recv_sem=a_recv.at[sem],
            device_id=device(*there),
            device_id_type=MESH,
        )

    for d in range(1, 4):
        there = moved(here, d, 0, 0)
        halves(there[0])
        quarter(left, left_in.at[here[0]], there[0], 0, there).start()
    halves(here[0])
    for d in range(1, 4):
        there = moved(here, 0, d, 0)
        quarter(right, right_in.at[here[1]], there[1], 1, there).start()

    def plane_sum(held, arrived, mine, target):
        def step(q, carry):
            value = held[mine * 16 + q].astype(F32)
            for d in range(1, 4):
                value = value + arrived[(mine + d) % 4, q].astype(F32)
            target[q] = value.astype(BF16)
            return carry

        lax.fori_loop(0, 16, step, 0, unroll=2)

    def scatter(source, target, sem, own, place_of):
        def step(k, carry):
            q = (own + k * 7) % 16
            pltpu.make_async_remote_copy(
                src_ref=source.at[q],
                dst_ref=target.at[own],
                send_sem=b_send.at[sem],
                recv_sem=b_recv.at[sem],
                device_id=device(*place_of(q // 4, q % 4)),
                device_id_type=MESH,
            ).start()
            return carry

        lax.fori_loop(1, 16, step, 0)
        target[own] = source[own]

    def three(buffer, sem):
        part = buffer.at[pl.ds(0, 3)]
        pltpu.make_async_copy(part, part, sem).wait()

    def fifteen(buffer, sem):
        part = buffer.at[pl.ds(0, 15)]
        pltpu.make_async_copy(part, part, sem).wait()

    three(left_in, a_recv.at[0])
    plane_sum(left, left_in, here[0], left_sum)
    scatter(left_sum, left_all, 0, here[1] * 4 + here[2], lambda a, b: (here[0], a, b, core))
    three(right_in, a_recv.at[1])
    plane_sum(right, right_in, here[1], right_sum)
    scatter(right_sum, right_all, 1, here[0] * 4 + here[2], lambda a, b: (a, here[1], b, core))

    for i in range(CHUNKS):
        wait_all(home.at[i], out_recv.at[i])
        pltpu.make_async_copy(back.at[i, me], home.at[i, me], own_sem.at[i]).wait()
    for n, buffer in enumerate((left_all, right_all)):
        fifteen(buffer, b_recv.at[n])
        value = buffer[0].astype(F32)
        for q in range(1, 16):
            value = value + buffer[q].astype(F32)
        total_ref[:, n * (D // 2) : (n + 1) * (D // 2)] = value

    cross.wait_send()
    for i in range(CHUNKS):
        wait_all(sent.at[i], in_send.at[i])
        wait_all(back.at[i], out_send.at[i])
    three(left_in, a_send.at[0])
    three(right_in, a_send.at[1])
    fifteen(left_all, b_send.at[0])
    fifteen(right_all, b_send.at[1])


def finish(home, total, gt, gw, gwo):
    def cells(b, carry):
        p = pl.ds(b, 1)
        blocks = [home[i, p][0].astype(F32) for i in range(CHUNKS)]
        value = jnp.concatenate([unfold(block, NW) for block in blocks], axis=0)
        gt[b // 4, pl.ds(pl.multiple_of((b % 4) * 16, 16), 16)] = value.astype(BF16)
        return carry

    lax.fori_loop(0, home.shape[1], cells, 0, unroll=4)

    @pl.when(pl.program_id(0) == 0)
    def _():
        scaled = total[...] * FACTOR
        for n in range(3):
            gw[:, n * D : (n + 1) * D] = scaled[n * 4 : (n + 1) * 4]
        gwo[...] = scaled[12:]


def body(tokens, cotangent, w_qkv, w_out):
    rows, columns, _ = tokens.shape
    vmem = pltpu.VMEM
    dma = pltpu.SemaphoreType.DMA
    regular = pltpu.SemaphoreType.REGULAR
    home, total = pl.pallas_call(
        kernel,
        out_shape=(
            jax.ShapeDtypeStruct((CHUNKS, CHIPS, 16, OUT_LANES), BF16),
            jax.ShapeDtypeStruct((16, D), F32),
        ),
        in_specs=[pl.BlockSpec(memory_space=pl.ANY)] * 4,
        out_specs=[pl.BlockSpec(memory_space=pl.ANY), pl.BlockSpec(memory_space=vmem)],
        scratch_shapes=[
            vmem((rows, columns, D), BF16),
            vmem((rows, columns, D), BF16),
            vmem((D, 3 * D), BF16),
            vmem((D, D), BF16),
            vmem((CHUNKS, CHIPS, 16, IN_LANES), BF16),
            vmem((CHUNKS, CHIPS, 16, IN_LANES), BF16),
            vmem((4, 2 * ROWS, 128), F32),
            vmem((ROWS, D), F32),
            vmem((ROWS, 128), F32),
            vmem((KEEP * ROWS, D), BF16),
            vmem((KEEP * ROWS, D), BF16),
            vmem((ROWS, 3 * D), BF16),
            vmem((ROWS, D), BF16),
            vmem((KEEP * ROWS, D), BF16),
            vmem((KEEP * ROWS, 3 * D), BF16),
            vmem((ROWS, D), F32),
            vmem((4, ROWS, 128), F32),
            vmem((CHUNKS, CHIPS, 16, OUT_LANES), BF16),
            vmem((D, 3 * D), F32),
            vmem((D, D), F32),
            vmem((8, 32, 4 * D), BF16),
            vmem((8, 32, 4 * D), BF16),
            vmem((CHIPS, 16, D // 2), BF16),
            vmem((CHIPS, 16, D // 2), BF16),
            vmem((4, 16, 16, D // 2), BF16),
            vmem((4, 16, 16, D // 2), BF16),
            vmem((16, 16, D // 2), BF16),
            vmem((16, 16, D // 2), BF16),
            vmem((16, 16, D // 2), BF16),
            vmem((16, 16, D // 2), BF16),
            dma((4,)), regular, regular, dma((CHUNKS,)),
            dma((CHUNKS,)), dma((CHUNKS,)),
            dma((CHUNKS,)), dma((CHUNKS,)),
            dma(()), dma(()),
            dma((2,)), dma((2,)),
            dma((2,)), dma((2,)),
        ],
        compiler_params=pltpu.CompilerParams(
            collective_id=0, has_side_effects=True, vmem_limit_bytes=60 << 20
        ),
        name="grid_attention_backward",
    )(tokens, cotangent, w_qkv, w_out)
    steps = 2
    return pl.pallas_call(
        finish,
        grid=(steps,),
        out_shape=(
            jax.ShapeDtypeStruct((rows, columns, D), BF16),
            jax.ShapeDtypeStruct((4, 3 * D), F32),
            jax.ShapeDtypeStruct((4, D), F32),
        ),
        in_specs=[
            pl.BlockSpec((CHUNKS, CHIPS // steps, 16, OUT_LANES), lambda s: (0, s, 0, 0)),
            pl.BlockSpec((16, D), lambda s: (0, 0)),
        ],
        out_specs=[
            pl.BlockSpec((rows // steps, columns, D), lambda s: (s, 0, 0)),
            pl.BlockSpec((4, 3 * D), lambda s: (0, 0)),
            pl.BlockSpec((4, D), lambda s: (0, 0)),
        ],
        compiler_params=pltpu.CompilerParams(vmem_limit_bytes=60 << 20),
        name="cells_from_blocks",
    )(home, total)


def solution(mesh):
    in_specs = (P("gy", "gx", None), P("gy", "gx", None), P(), P())
    out_specs = (P("gy", "gx", None), P(("gy", "gx"), None), P(("gy", "gx"), None))
    return jax.shard_map(body, mesh=mesh, in_specs=in_specs, out_specs=out_specs, check_vma=False)
```

```python
import random

import jax
import jax.numpy as jnp
from jax import lax
from jax.experimental import pallas as pl
from jax.experimental.pallas import tpu as pltpu
from jax.sharding import PartitionSpec as P

MESH = pl.DeviceIdType.MESH
F32 = jnp.float32
BF16 = jnp.bfloat16

D = 512
HEAD = 32
EPS = 1e-05
CHIPS = 64
MEMBERS = 64
WINDOWS = 16
CHUNKS = 4
NW = WINDOWS // CHUNKS
ROWS = NW * MEMBERS
KEEP = CHUNKS // 2
IN_LANES = 2 * NW * D // 16
OUT_LANES = NW * D // 16
TOGETHER = 4
SCALE = HEAD ** (-0.5)
LOG2E = 1.4426950408889634
FACTOR = 131072.0 ** (-0.5)


def place():
    gy = lax.axis_index("gy")
    gx = lax.axis_index("gx")
    return gy // 4, (gx // 4) * 2 + (gy // 2) % 2, gx % 4, gy % 2


def device(x, y, z, core):
    return (x * 4 + (y % 2) * 2 + core, (y // 2) * 4 + z)


def chip_of(x, y, z):
    return x * 16 + y * 4 + z


def moved(here, x, y, z):
    return (here[0] + x) % 4, (here[1] + y) % 4, (here[2] + z) % 4, here[3]


SHIFTS = [(k // 16, (k // 4) % 4, k % 4) for k in range(1, CHIPS)]
random.Random(1).shuffle(SHIFTS)
PLANE_SHIFTS = [(s[1], s[2]) for s in SHIFTS if s[0] == 0]
LINE, PLANE, SPACE = ([s for s in SHIFTS if 3 - s.count(0) == n] for n in (1, 2, 3))


class Places:
    def __init__(self, here):
        along = [[(here[a] + d) % 4 for d in range(4)] for a in range(3)]
        self.core = here[3]
        self.along = along
        self.x_chip = [x * 16 for x in along[0]]
        self.x_gy = [x * 4 + self.core for x in along[0]]
        self.y_chip = [y * 4 for y in along[1]]
        self.y_gy = [(y % 2) * 2 for y in along[1]]
        self.y_gx = [(y // 2) * 4 for y in along[1]]
        self.z = along[2]

    def chip(self, s):
        return self.x_chip[s[0]] + (self.y_chip[s[1]] + self.z[s[2]])

    def at(self, s):
        return [self.along[a][s[a]] for a in range(3)]

    def device(self, s):
        return self.x_gy[s[0]] + self.y_gy[s[1]], self.y_gx[s[1]] + self.z[s[2]]


def send(places, shifts, source, target, send_sem, recv_sem):
    me = places.chip((0, 0, 0))
    landing = target.at[me]
    for s in shifts:
        pltpu.make_async_remote_copy(
            src_ref=source.at[places.chip(s)],
            dst_ref=landing,
            send_sem=send_sem,
            recv_sem=recv_sem,
            device_id=places.device(s),
            device_id_type=MESH,
        ).start()


def wait_all(buffer, sem):
    part = buffer.at[pl.ds(0, CHIPS - 1)]
    pltpu.make_async_copy(part, part, sem).wait()


def dot(a, b):
    return jnp.dot(a, b, preferred_element_type=F32)


def dot_t(a, b):
    return lax.dot_general(a, b, (((1,), (1,)), ((), ())), preferred_element_type=F32)


def dot_0(a, b):
    return lax.dot_general(a, b, (((0,), (0,)), ((), ())), preferred_element_type=F32)


def fold(rows):
    n, width = rows.shape
    parts = 16 // n
    lanes = width // parts
    return jnp.concatenate([rows[:, i * lanes : (i + 1) * lanes] for i in range(parts)], axis=0)


def unfold(block, n):
    parts = 16 // n
    return jnp.concatenate([block[i * n : (i + 1) * n] for i in range(parts)], axis=1)


def attend(w, base, qkv, gatt, dqkv, att):
    lane = lax.broadcasted_iota(jnp.int32, (MEMBERS, 128), 1) // HEAD
    zero = jnp.zeros((MEMBERS, 128), BF16)

    def spread(a):
        return jnp.concatenate([jnp.where(lane == h, a, zero) for h in range(4)], axis=0)

    def diagonal(blocks):
        total = blocks[3 * MEMBERS :]
        for h in range(3):
            total = jnp.where(lane == h, blocks[h * MEMBERS : (h + 1) * MEMBERS], total)
        return total.astype(BF16)

    units = []
    for i in range(TOGETHER):
        start = (w * TOGETHER + i) * MEMBERS
        inside = pl.ds(pl.multiple_of(start, MEMBERS), MEMBERS)
        kept = pl.ds(pl.multiple_of(base + start, MEMBERS), MEMBERS)
        for g in range(4):
            units.append((inside, kept, [slice(n * D + g * 128, n * D + (g + 1) * 128) for n in range(3)]))
    qs = [spread(qkv[r, c[0]]) for r, _, c in units]
    gs = [spread(gatt[r, c[0]]) for r, _, c in units]
    s = [dot_t(qkv[r, c[1]], b) * (SCALE * LOG2E) for (r, _, c), b in zip(units, qs)]
    gp = [dot_t(qkv[r, c[2]], b) for (r, _, c), b in zip(units, gs)]
    e = [jnp.exp2(a - jnp.max(a, axis=0, keepdims=True)) for a in s]
    p = [a * (1.0 / jnp.sum(a, axis=0, keepdims=True)) for a in e]
    low = [a.astype(BF16) for a in p]
    ds = [
        (a * (b - jnp.sum(a * b, axis=0, keepdims=True)) * SCALE).astype(BF16)
        for a, b in zip(p, gp)
    ]
    for n, (r, kept, c) in enumerate(units):
        dqkv[kept, c[1]] = dot(ds[n], qs[n]).astype(BF16)
        dqkv[kept, c[2]] = dot(low[n], gs[n]).astype(BF16)
    for n, (r, kept, c) in enumerate(units):
        att[kept, c[0]] = diagonal(dot_0(low[n], qkv[r, c[2]]))
        dqkv[kept, c[0]] = diagonal(dot_0(ds[n], qkv[r, c[1]]))


def kernel(
    tok_hbm, cot_hbm, wqkv_hbm, wout_hbm,
    home, total_ref,
    tok, cot, wqkv, wout,
    sent, got, both_f, xhat, rstd, normed, cot_w, qkv, gatt, att, dqkv, gnorm, back_f,
    back, dw, given, taken,
    parts, line_in, line_sum, plane_in, straight,
    load_sem, line_sem, space_sem, own_sem,
    in_send, in_recv, out_send, out_recv, x_send, x_recv, a_send, a_recv, b_send, b_recv, r_send, r_recv,
):
    here = place()
    core = here[3]
    places = Places(here)
    me = chip_of(*here[:3])
    partner = device(here[0], here[1], here[2], 1 - core)

    loads = [
        pltpu.make_async_copy(tok_hbm, tok, load_sem.at[0]),
        pltpu.make_async_copy(cot_hbm, cot, load_sem.at[1]),
        pltpu.make_async_copy(wqkv_hbm, wqkv, load_sem.at[2]),
        pltpu.make_async_copy(wout_hbm, wout, load_sem.at[3]),
    ]
    for load in loads:
        load.start()

    barrier = pltpu.get_barrier_semaphore()

    def signal(sem, shifts):
        for s in shifts:
            pl.semaphore_signal(sem, inc=1, device_id=places.device(s), device_id_type=MESH)

    signal(barrier, LINE)
    pl.semaphore_signal(barrier, inc=1, device_id=partner, device_id_type=MESH)
    loads[0].wait()
    loads[1].wait()

    def pack(p, carry):
        cells = (p // 4, pl.ds(pl.multiple_of((p % 4) * 16, 16), 16))
        t = tok[cells].astype(F32)
        c = cot[cells].astype(F32)
        for i in range(CHUNKS):
            rows = slice(i * NW, (i + 1) * NW)
            sent[i, p] = fold(jnp.concatenate([t[rows], c[rows]], axis=0)).astype(BF16)
        return carry

    lax.fori_loop(0, CHIPS, pack, 0, unroll=2)
    for i in range(CHUNKS):
        got[i, me] = sent[i, me]

    def send_in(i, shifts):
        send(places, shifts, sent.at[i], got.at[i], in_send.at[i], in_recv.at[i])

    pl.semaphore_wait(barrier, 10)
    signal(line_sem, LINE)
    for i in range(2):
        send_in(i, LINE)
    pl.semaphore_wait(line_sem, 9)
    signal(space_sem, [(d, 0, 0) for d in range(1, 4)])
    send_in(0, PLANE)
    pl.semaphore_wait(space_sem, 3)
    send_in(0, SPACE)
    send_in(1, PLANE + SPACE)
    for i in range(2, CHUNKS):
        send_in(i, SHIFTS)
    def cross(n):
        return pltpu.make_async_remote_copy(
            src_ref=given.at[n],
            dst_ref=taken.at[n],
            send_sem=x_send.at[n],
            recv_sem=x_recv.at[n],
            device_id=partner,
            device_id_type=MESH,
        )

    def send_out(i):
        def repack(b, carry):
            rows = pl.ds(pl.multiple_of(b * 8, 8), 8)
            block = jnp.concatenate([back_f[t, rows, :] for t in range(4)], axis=1)
            for k in range(8 // NW):
                back[i, b * (8 // NW) + k] = fold(block[k * NW : (k + 1) * NW]).astype(BF16)
            return carry

        lax.fori_loop(0, ROWS // 8, repack, 0, unroll=2)
        send(places, SHIFTS, back.at[i], home.at[i], out_send.at[i], out_recv.at[i])
        pltpu.make_async_copy(back.at[i, me], home.at[i, me], own_sem.at[i]).start()

    loads[2].wait()
    loads[3].wait()

    for i in range(CHUNKS):
        wait_all(got.at[i], in_recv.at[i])
        base = (i % KEEP) * ROWS
        kept = slice(base, base + ROWS)

        def unpack(p, carry):
            block = unfold(got[i, p].astype(F32), 2 * NW) if NW < 8 else got[i, p].astype(F32)
            rows = pl.ds(pl.multiple_of(p * 2 * NW, 8), 2 * NW)
            for t in range(4):
                both_f[t, rows, :] = block[:, t * 128 : (t + 1) * 128]
            return carry

        lax.fori_loop(0, CHIPS, unpack, 0, unroll=4)

        for j in range(NW):
            window = slice(j * MEMBERS, (j + 1) * MEMBERS)
            members = pl.ds(j, MEMBERS, stride=2 * NW)
            values = jnp.concatenate([both_f[t, members, :] for t in range(4)], axis=1)
            mean = jnp.mean(values, axis=-1, keepdims=True)
            centred = values - mean
            variance = jnp.mean(centred * centred, axis=-1, keepdims=True)
            inverse = lax.rsqrt(variance + EPS)
            standard = centred * inverse
            xhat[window, :] = standard
            rstd[window, :] = jnp.broadcast_to(inverse, (MEMBERS, 128))
            low = slice(base + j * MEMBERS, base + (j + 1) * MEMBERS)
            normed[low, :] = standard.astype(BF16)
            members = pl.ds(NW + j, MEMBERS, stride=2 * NW)
            cot_w[low, :] = jnp.concatenate(
                [both_f[t, members, :] for t in range(4)], axis=1
            ).astype(BF16)

        for n in range(3):
            columns = slice(n * D, (n + 1) * D)
            qkv[:, columns] = dot(normed[kept, :], wqkv[:, columns]).astype(BF16)
        gatt[...] = dot_t(cot_w[kept, :], wout[...]).astype(BF16)

        def attention(w, carry):
            attend(w, base, qkv, gatt, dqkv, att)
            return carry

        lax.fori_loop(0, NW // TOGETHER, attention, 0)

        if i % KEEP == KEEP - 1:
            for n in range(4):
                columns = slice(n * D, (n + 1) * D)
                if n < 3:
                    term = dot_0(normed[...], dqkv[:, columns])
                else:
                    term = dot_0(att[...], cot_w[...])
                dw[:, columns] = term if i < KEEP else dw[:, columns] + term
                if i == CHUNKS - 1:
                    for b in range(8):
                        rows = pl.ds(pl.multiple_of(b * 64 + (1 - core) * 32, 32), 32)
                        given[n, b] = dw[rows, columns].astype(BF16)
                    cross(n).start()

        gnorm[...] = dot_t(dqkv[kept, :], wqkv[...])
        for j in range(NW):
            window = slice(j * MEMBERS, (j + 1) * MEMBERS)
            members = pl.ds(j, MEMBERS, stride=NW)
            g = gnorm[window, :]
            standard = xhat[window, :]
            average = jnp.mean(g, axis=-1, keepdims=True)
            projected = jnp.mean(g * standard, axis=-1, keepdims=True)
            layer = rstd[window, 0:1] * (g - average - standard * projected)
            result = cot_w[base + j * MEMBERS : base + (j + 1) * MEMBERS, :].astype(F32) + layer
            for t in range(4):
                back_f[t, members, :] = result[:, t * 128 : (t + 1) * 128]

        if i < CHUNKS - 1:
            send_out(i)

    send_out(CHUNKS - 1)
    for n in range(4):
        cross(n).wait_recv()

    def halves(owner_x):
        def step(b, carry):
            y_lo, y_hi = b // 2, b % 2
            block = owner_x * 2 + y_lo
            rows = pl.ds(pl.multiple_of(block * 64 + core * 32 + y_hi * 16, 16), 16)
            half = pl.ds(pl.multiple_of(y_hi * 16, 16), 16)
            mine = [
                dw[rows, n * D : (n + 1) * D] + taken[n, block, half, :].astype(F32) for n in range(4)
            ]
            y = y_hi * 2 + y_lo
            for z in range(4):
                piece = jnp.concatenate([m[z * 4 : (z + 1) * 4] for m in mine], axis=0).astype(BF16)
                chip = owner_x * 16 + y * 4 + z
                slots = (chip, y * 16 + owner_x * 4 + z, z * 16 + owner_x * 4 + y, chip)
                for a in range(4):
                    parts[a, slots[a]] = piece[:, a * 128 : (a + 1) * 128]
            return carry

        lax.fori_loop(0, 4, step, 0)

    def along(a, d):
        there = moved(here, *(d if n == a else 0 for n in range(3)))
        pltpu.make_async_remote_copy(
            src_ref=parts.at[a, pl.ds(pl.multiple_of(there[a] * 16, 16), 16)],
            dst_ref=line_in.at[a, here[a]],
            send_sem=a_send.at[a],
            recv_sem=a_recv.at[a],
            device_id=device(*there),
            device_id_type=MESH,
        ).start()

    for d in range(1, 4):
        halves((here[0] + d) % 4)
        along(0, d)
    halves(here[0])
    for d in range(1, 4):
        along(1, d)
        along(2, d)
    send(places, SHIFTS, parts.at[3], straight, r_send, r_recv)
    straight[me] = parts[3, me]

    def three(buffer, sem):
        part = buffer.at[pl.ds(0, 3)]
        pltpu.make_async_copy(part, part, sem).wait()

    def fifteen(buffer, sem):
        part = buffer.at[pl.ds(0, 15)]
        pltpu.make_async_copy(part, part, sem).wait()

    across = ((1, 2), (0, 2), (0, 1))
    for a in range(3):
        three(line_in.at[a], a_recv.at[a])
        p, q = across[a]

        def plane_sum(k, carry):
            value = parts[a, here[a] * 16 + k].astype(F32)
            for d in range(1, 4):
                value = value + line_in[a, (here[a] + d) % 4, k].astype(F32)
            line_sum[a, k] = value.astype(BF16)
            return carry

        lax.fori_loop(0, 16, plane_sum, 0, unroll=4)
        own = here[p] * 4 + here[q]
        landing = plane_in.at[a, own]
        for s in PLANE_SHIFTS:
            shift = [0, 0, 0]
            shift[p], shift[q] = s
            there = places.at(shift)
            pltpu.make_async_remote_copy(
                src_ref=line_sum.at[a, there[p] * 4 + there[q]],
                dst_ref=landing,
                send_sem=b_send.at[a],
                recv_sem=b_recv.at[a],
                device_id=places.device(shift),
                device_id_type=MESH,
            ).start()
        plane_in[a, own] = line_sum[a, own]

    for i in range(CHUNKS):
        wait_all(home.at[i], out_recv.at[i])
        pltpu.make_async_copy(back.at[i, me], home.at[i, me], own_sem.at[i]).wait()
    wait_all(straight, r_recv)

    def add(k, acc):
        for n in range(8):
            acc = acc + straight[k * 8 + n].astype(F32)
        return acc

    total_ref[:, 3 * 128 :] = lax.fori_loop(0, CHIPS // 8, add, jnp.zeros((16, 128), F32))
    for a in range(3):
        fifteen(plane_in.at[a], b_recv.at[a])
        value = plane_in[a, 0].astype(F32)
        for k in range(1, 16):
            value = value + plane_in[a, k].astype(F32)
        total_ref[:, a * 128 : (a + 1) * 128] = value

    for n in range(4):
        cross(n).wait_send()
    for i in range(CHUNKS):
        wait_all(sent.at[i], in_send.at[i])
        wait_all(back.at[i], out_send.at[i])
    for a in range(3):
        three(line_in.at[a], a_send.at[a])
        fifteen(plane_in.at[a], b_send.at[a])
    wait_all(straight, r_send)


def finish(home, total, gt, gw, gwo):
    def cells(b, carry):
        p = pl.ds(b, 1)
        blocks = [home[i, p][0].astype(F32) for i in range(CHUNKS)]
        value = jnp.concatenate([unfold(block, NW) for block in blocks], axis=0)
        gt[b // 4, pl.ds(pl.multiple_of((b % 4) * 16, 16), 16)] = value.astype(BF16)
        return carry

    lax.fori_loop(0, home.shape[1], cells, 0, unroll=4)

    @pl.when(pl.program_id(0) == 0)
    def _():
        scaled = total[...] * FACTOR
        for n in range(3):
            gw[:, n * D : (n + 1) * D] = scaled[n * 4 : (n + 1) * 4]
        gwo[...] = scaled[12:]


def body(tokens, cotangent, w_qkv, w_out):
    rows, columns, _ = tokens.shape
    vmem = pltpu.VMEM
    dma = pltpu.SemaphoreType.DMA
    regular = pltpu.SemaphoreType.REGULAR
    home, total = pl.pallas_call(
        kernel,
        out_shape=(
            jax.ShapeDtypeStruct((CHUNKS, CHIPS, 16, OUT_LANES), BF16),
            jax.ShapeDtypeStruct((16, D), F32),
        ),
        in_specs=[pl.BlockSpec(memory_space=pl.ANY)] * 4,
        out_specs=[pl.BlockSpec(memory_space=pl.ANY), pl.BlockSpec(memory_space=vmem)],
        scratch_shapes=[
            vmem((rows, columns, D), BF16),
            vmem((rows, columns, D), BF16),
            vmem((D, 3 * D), BF16),
            vmem((D, D), BF16),
            vmem((CHUNKS, CHIPS, 16, IN_LANES), BF16),
            vmem((CHUNKS, CHIPS, 16, IN_LANES), BF16),
            vmem((4, 2 * ROWS, 128), F32),
            vmem((ROWS, D), F32),
            vmem((ROWS, 128), F32),
            vmem((KEEP * ROWS, D), BF16),
            vmem((KEEP * ROWS, D), BF16),
            vmem((ROWS, 3 * D), BF16),
            vmem((ROWS, D), BF16),
            vmem((KEEP * ROWS, D), BF16),
            vmem((KEEP * ROWS, 3 * D), BF16),
            vmem((ROWS, D), F32),
            vmem((4, ROWS, 128), F32),
            vmem((CHUNKS, CHIPS, 16, OUT_LANES), BF16),
            vmem((D, 4 * D), F32),
            vmem((4, 8, 32, D), BF16),
            vmem((4, 8, 32, D), BF16),
            vmem((4, CHIPS, 16, 128), BF16),
            vmem((3, 4, 16, 16, 128), BF16),
            vmem((3, 16, 16, 128), BF16),
            vmem((3, 16, 16, 128), BF16),
            vmem((CHIPS, 16, 128), BF16),
            dma((4,)), regular, regular, dma((CHUNKS,)),
            dma((CHUNKS,)), dma((CHUNKS,)),
            dma((CHUNKS,)), dma((CHUNKS,)),
            dma((4,)), dma((4,)),
            dma((3,)), dma((3,)),
            dma((3,)), dma((3,)),
            dma(()), dma(()),
        ],
        compiler_params=pltpu.CompilerParams(
            collective_id=0, has_side_effects=True, vmem_limit_bytes=60 << 20
        ),
        name="grid_attention_backward",
    )(tokens, cotangent, w_qkv, w_out)
    steps = 2
    return pl.pallas_call(
        finish,
        grid=(steps,),
        out_shape=(
            jax.ShapeDtypeStruct((rows, columns, D), BF16),
            jax.ShapeDtypeStruct((4, 3 * D), F32),
            jax.ShapeDtypeStruct((4, D), F32),
        ),
        in_specs=[
            pl.BlockSpec((CHUNKS, CHIPS // steps, 16, OUT_LANES), lambda s: (0, s, 0, 0)),
            pl.BlockSpec((16, D), lambda s: (0, 0)),
        ],
        out_specs=[
            pl.BlockSpec((rows // steps, columns, D), lambda s: (s, 0, 0)),
            pl.BlockSpec((4, 3 * D), lambda s: (0, 0)),
            pl.BlockSpec((4, D), lambda s: (0, 0)),
        ],
        compiler_params=pltpu.CompilerParams(vmem_limit_bytes=60 << 20),
        name="cells_from_blocks",
    )(home, total)


def solution(mesh):
    in_specs = (P("gy", "gx", None), P("gy", "gx", None), P(), P())
    out_specs = (P("gy", "gx", None), P(("gy", "gx"), None), P(("gy", "gx"), None))
    return jax.shard_map(body, mesh=mesh, in_specs=in_specs, out_specs=out_specs, check_vma=False)
```

```python
import random

import jax
import jax.numpy as jnp
from jax import lax
from jax.experimental import pallas as pl
from jax.experimental.pallas import tpu as pltpu
from jax.sharding import PartitionSpec as P

MESH = pl.DeviceIdType.MESH
F32 = jnp.float32
BF16 = jnp.bfloat16

D = 512
HEAD = 32
EPS = 1e-05
CHIPS = 64
MEMBERS = 64
WINDOWS = 16
CHUNKS = 4
NW = WINDOWS // CHUNKS
ROWS = NW * MEMBERS
KEEP = CHUNKS // 2
IN_LANES = 2 * NW * D // 16
OUT_LANES = NW * D // 16
TOGETHER = 4
SCALE = HEAD ** (-0.5)
LOG2E = 1.4426950408889634
FACTOR = 131072.0 ** (-0.5)


def place():
    gy = lax.axis_index("gy")
    gx = lax.axis_index("gx")
    return gy // 4, (gx // 4) * 2 + (gy // 2) % 2, gx % 4, gy % 2


def device(x, y, z, core):
    return (x * 4 + (y % 2) * 2 + core, (y // 2) * 4 + z)


def chip_of(x, y, z):
    return x * 16 + y * 4 + z


def moved(here, x, y, z):
    return (here[0] + x) % 4, (here[1] + y) % 4, (here[2] + z) % 4, here[3]


SHIFTS = [(k // 16, (k // 4) % 4, k % 4) for k in range(1, CHIPS)]
random.Random(1).shuffle(SHIFTS)
PLANE_SHIFTS = [(s[1], s[2]) for s in SHIFTS if s[0] == 0]
LINE, PLANE, SPACE = ([s for s in SHIFTS if 3 - s.count(0) == n] for n in (1, 2, 3))


class Places:
    def __init__(self, here):
        along = [[(here[a] + d) % 4 for d in range(4)] for a in range(3)]
        self.core = here[3]
        self.along = along
        self.x_chip = [x * 16 for x in along[0]]
        self.x_gy = [x * 4 + self.core for x in along[0]]
        self.y_chip = [y * 4 for y in along[1]]
        self.y_gy = [(y % 2) * 2 for y in along[1]]
        self.y_gx = [(y // 2) * 4 for y in along[1]]
        self.z = along[2]

    def chip(self, s):
        return self.x_chip[s[0]] + (self.y_chip[s[1]] + self.z[s[2]])

    def at(self, s):
        return [self.along[a][s[a]] for a in range(3)]

    def device(self, s):
        return self.x_gy[s[0]] + self.y_gy[s[1]], self.y_gx[s[1]] + self.z[s[2]]


def send(places, shifts, source, target, send_sem, recv_sem):
    me = places.chip((0, 0, 0))
    landing = target.at[me]
    for s in shifts:
        pltpu.make_async_remote_copy(
            src_ref=source.at[places.chip(s)],
            dst_ref=landing,
            send_sem=send_sem,
            recv_sem=recv_sem,
            device_id=places.device(s),
            device_id_type=MESH,
        ).start()


def wait_all(buffer, sem):
    part = buffer.at[pl.ds(0, CHIPS - 1)]
    pltpu.make_async_copy(part, part, sem).wait()


def dot(a, b):
    return jnp.dot(a, b, preferred_element_type=F32)


def dot_t(a, b):
    return lax.dot_general(a, b, (((1,), (1,)), ((), ())), preferred_element_type=F32)


def dot_0(a, b):
    return lax.dot_general(a, b, (((0,), (0,)), ((), ())), preferred_element_type=F32)


def fold(rows):
    n, width = rows.shape
    parts = 16 // n
    lanes = width // parts
    return jnp.concatenate([rows[:, i * lanes : (i + 1) * lanes] for i in range(parts)], axis=0)


def unfold(block, n):
    parts = 16 // n
    return jnp.concatenate([block[i * n : (i + 1) * n] for i in range(parts)], axis=1)


def attend(w, base, qkv, gatt, dqkv, att):
    lane = lax.broadcasted_iota(jnp.int32, (MEMBERS, 128), 1) // HEAD
    zero = jnp.zeros((MEMBERS, 128), BF16)

    def spread(a):
        return jnp.concatenate([jnp.where(lane == h, a, zero) for h in range(4)], axis=0)

    def diagonal(blocks):
        total = blocks[3 * MEMBERS :]
        for h in range(3):
            total = jnp.where(lane == h, blocks[h * MEMBERS : (h + 1) * MEMBERS], total)
        return total.astype(BF16)

    units = []
    for i in range(TOGETHER):
        start = (w * TOGETHER + i) * MEMBERS
        inside = pl.ds(pl.multiple_of(start, MEMBERS), MEMBERS)
        kept = pl.ds(pl.multiple_of(base + start, MEMBERS), MEMBERS)
        for g in range(4):
            units.append((inside, kept, [slice(n * D + g * 128, n * D + (g + 1) * 128) for n in range(3)]))
    qs = [spread(qkv[r, c[0]]) for r, _, c in units]
    gs = [spread(gatt[r, c[0]]) for r, _, c in units]
    s = [dot_t(qkv[r, c[1]], b) * (SCALE * LOG2E) for (r, _, c), b in zip(units, qs)]
    gp = [dot_t(qkv[r, c[2]], b) for (r, _, c), b in zip(units, gs)]
    e = [jnp.exp2(a - jnp.max(a, axis=0, keepdims=True)) for a in s]
    p = [a * (1.0 / jnp.sum(a, axis=0, keepdims=True)) for a in e]
    low = [a.astype(BF16) for a in p]
    ds = [
        (a * (b - jnp.sum(a * b, axis=0, keepdims=True)) * SCALE).astype(BF16)
        for a, b in zip(p, gp)
    ]
    for n, (r, kept, c) in enumerate(units):
        dqkv[kept, c[1]] = dot(ds[n], qs[n]).astype(BF16)
        dqkv[kept, c[2]] = dot(low[n], gs[n]).astype(BF16)
    for n, (r, kept, c) in enumerate(units):
        att[kept, c[0]] = diagonal(dot_0(low[n], qkv[r, c[2]]))
        dqkv[kept, c[0]] = diagonal(dot_0(ds[n], qkv[r, c[1]]))


def kernel(
    tok_hbm, cot_hbm, wqkv_hbm, wout_hbm,
    home, total_ref,
    tok, cot, wqkv, wout,
    sent, got, both_f, xhat, rstd, normed, cot_w, qkv, gatt, att, dqkv, gnorm, back_f,
    back, dw, given, taken,
    parts, line_in, line_sum, plane_in, straight,
    load_sem, line_sem, space_sem, own_sem,
    in_send, in_recv, out_send, out_recv, x_send, x_recv, a_send, a_recv, b_send, b_recv, r_send, r_recv,
):
    here = place()
    core = here[3]
    places = Places(here)
    me = chip_of(*here[:3])
    partner = device(here[0], here[1], here[2], 1 - core)

    loads = [
        pltpu.make_async_copy(tok_hbm, tok, load_sem.at[0]),
        pltpu.make_async_copy(cot_hbm, cot, load_sem.at[1]),
        pltpu.make_async_copy(wqkv_hbm, wqkv, load_sem.at[2]),
        pltpu.make_async_copy(wout_hbm, wout, load_sem.at[3]),
    ]
    for load in loads:
        load.start()

    barrier = pltpu.get_barrier_semaphore()

    def signal(sem, shifts):
        for s in shifts:
            pl.semaphore_signal(sem, inc=1, device_id=places.device(s), device_id_type=MESH)

    signal(barrier, LINE)
    pl.semaphore_signal(barrier, inc=1, device_id=partner, device_id_type=MESH)
    loads[0].wait()
    loads[1].wait()

    def pack(p, carry):
        cells = (p // 4, pl.ds(pl.multiple_of((p % 4) * 16, 16), 16))
        t = tok[cells].astype(F32)
        c = cot[cells].astype(F32)
        for i in range(CHUNKS):
            rows = slice(i * NW, (i + 1) * NW)
            sent[i, p] = fold(jnp.concatenate([t[rows], c[rows]], axis=0)).astype(BF16)
        return carry

    lax.fori_loop(0, CHIPS, pack, 0, unroll=2)
    for i in range(CHUNKS):
        got[i, me] = sent[i, me]

    def send_in(i, shifts):
        send(places, shifts, sent.at[i], got.at[i], in_send.at[i], in_recv.at[i])

    pl.semaphore_wait(barrier, 10)
    signal(line_sem, LINE)
    for i in range(CHUNKS):
        send_in(i, LINE)
    pl.semaphore_wait(line_sem, 9)
    signal(space_sem, [(d, 0, 0) for d in range(1, 4)])
    send_in(0, PLANE)
    pl.semaphore_wait(space_sem, 3)
    send_in(0, SPACE)
    for i in range(1, CHUNKS):
        send_in(i, PLANE + SPACE)
    def cross(n):
        return pltpu.make_async_remote_copy(
            src_ref=given.at[n],
            dst_ref=taken.at[n],
            send_sem=x_send.at[n],
            recv_sem=x_recv.at[n],
            device_id=partner,
            device_id_type=MESH,
        )

    def send_out(i):
        def repack(b, carry):
            rows = pl.ds(pl.multiple_of(b * 8, 8), 8)
            block = jnp.concatenate([back_f[t, rows, :] for t in range(4)], axis=1)
            for k in range(8 // NW):
                back[i, b * (8 // NW) + k] = fold(block[k * NW : (k + 1) * NW]).astype(BF16)
            return carry

        lax.fori_loop(0, ROWS // 8, repack, 0, unroll=2)
        send(places, SHIFTS, back.at[i], home.at[i], out_send.at[i], out_recv.at[i])
        pltpu.make_async_copy(back.at[i, me], home.at[i, me], own_sem.at[i]).start()

    loads[2].wait()
    loads[3].wait()

    for i in range(CHUNKS):
        wait_all(got.at[i], in_recv.at[i])
        base = (i % KEEP) * ROWS
        kept = slice(base, base + ROWS)

        def unpack(p, carry):
            block = unfold(got[i, p].astype(F32), 2 * NW) if NW < 8 else got[i, p].astype(F32)
            rows = pl.ds(pl.multiple_of(p * 2 * NW, 8), 2 * NW)
            for t in range(4):
                both_f[t, rows, :] = block[:, t * 128 : (t + 1) * 128]
            return carry

        lax.fori_loop(0, CHIPS, unpack, 0, unroll=4)

        for j in range(NW):
            window = slice(j * MEMBERS, (j + 1) * MEMBERS)
            members = pl.ds(j, MEMBERS, stride=2 * NW)
            values = jnp.concatenate([both_f[t, members, :] for t in range(4)], axis=1)
            mean = jnp.mean(values, axis=-1, keepdims=True)
            centred = values - mean
            variance = jnp.mean(centred * centred, axis=-1, keepdims=True)
            inverse = lax.rsqrt(variance + EPS)
            standard = centred * inverse
            xhat[window, :] = standard
            rstd[window, :] = jnp.broadcast_to(inverse, (MEMBERS, 128))
            low = slice(base + j * MEMBERS, base + (j + 1) * MEMBERS)
            normed[low, :] = standard.astype(BF16)
            members = pl.ds(NW + j, MEMBERS, stride=2 * NW)
            cot_w[low, :] = jnp.concatenate(
                [both_f[t, members, :] for t in range(4)], axis=1
            ).astype(BF16)

        for n in range(3):
            columns = slice(n * D, (n + 1) * D)
            qkv[:, columns] = dot(normed[kept, :], wqkv[:, columns]).astype(BF16)
        gatt[...] = dot_t(cot_w[kept, :], wout[...]).astype(BF16)

        def attention(w, carry):
            attend(w, base, qkv, gatt, dqkv, att)
            return carry

        lax.fori_loop(0, NW // TOGETHER, attention, 0)

        if i > 0:
            used = slice(0, (i + 1) * ROWS) if i < KEEP else kept
            for n in range(4):
                columns = slice(n * D, (n + 1) * D)
                if n < 3:
                    term = dot_0(normed[used, :], dqkv[used, columns])
                else:
                    term = dot_0(att[used, :], cot_w[used, :])
                dw[:, columns] = term if i < KEEP else dw[:, columns] + term
                if i == CHUNKS - 1:
                    for b in range(8):
                        rows = pl.ds(pl.multiple_of(b * 64 + (1 - core) * 32, 32), 32)
                        given[n, b] = dw[rows, columns].astype(BF16)
                    cross(n).start()

        gnorm[...] = dot_t(dqkv[kept, :], wqkv[...])
        for j in range(NW):
            window = slice(j * MEMBERS, (j + 1) * MEMBERS)
            members = pl.ds(j, MEMBERS, stride=NW)
            g = gnorm[window, :]
            standard = xhat[window, :]
            average = jnp.mean(g, axis=-1, keepdims=True)
            projected = jnp.mean(g * standard, axis=-1, keepdims=True)
            layer = rstd[window, 0:1] * (g - average - standard * projected)
            result = cot_w[base + j * MEMBERS : base + (j + 1) * MEMBERS, :].astype(F32) + layer
            for t in range(4):
                back_f[t, members, :] = result[:, t * 128 : (t + 1) * 128]

        if i < CHUNKS - 1:
            send_out(i)

    send_out(CHUNKS - 1)
    for n in range(4):
        cross(n).wait_recv()

    def halves(owner_x):
        def step(b, carry):
            y_lo, y_hi = b // 2, b % 2
            block = owner_x * 2 + y_lo
            rows = pl.ds(pl.multiple_of(block * 64 + core * 32 + y_hi * 16, 16), 16)
            half = pl.ds(pl.multiple_of(y_hi * 16, 16), 16)
            mine = [
                dw[rows, n * D : (n + 1) * D] + taken[n, block, half, :].astype(F32) for n in range(4)
            ]
            y = y_hi * 2 + y_lo
            for z in range(4):
                piece = jnp.concatenate([m[z * 4 : (z + 1) * 4] for m in mine], axis=0).astype(BF16)
                chip = owner_x * 16 + y * 4 + z
                slots = (chip, y * 16 + owner_x * 4 + z, z * 16 + owner_x * 4 + y, chip)
                for a in range(4):
                    parts[a, slots[a]] = piece[:, a * 128 : (a + 1) * 128]
            return carry

        lax.fori_loop(0, 4, step, 0, unroll=2)

    def along(a, d):
        there = moved(here, *(d if n == a else 0 for n in range(3)))
        pltpu.make_async_remote_copy(
            src_ref=parts.at[a, pl.ds(pl.multiple_of(there[a] * 16, 16), 16)],
            dst_ref=line_in.at[a, here[a]],
            send_sem=a_send.at[a],
            recv_sem=a_recv.at[a],
            device_id=device(*there),
            device_id_type=MESH,
        ).start()

    for d in range(1, 4):
        halves((here[0] + d) % 4)
        along(0, d)
    halves(here[0])
    for d in range(1, 4):
        along(1, d)
        along(2, d)
    send(places, SHIFTS, parts.at[3], straight, r_send, r_recv)
    straight[me] = parts[3, me]

    def three(buffer, sem):
        part = buffer.at[pl.ds(0, 3)]
        pltpu.make_async_copy(part, part, sem).wait()

    def fifteen(buffer, sem):
        part = buffer.at[pl.ds(0, 15)]
        pltpu.make_async_copy(part, part, sem).wait()

    across = ((1, 2), (0, 2), (0, 1))
    for a in range(3):
        three(line_in.at[a], a_recv.at[a])
        p, q = across[a]

        def plane_sum(k, carry):
            value = parts[a, here[a] * 16 + k].astype(F32)
            for d in range(1, 4):
                value = value + line_in[a, (here[a] + d) % 4, k].astype(F32)
            line_sum[a, k] = value.astype(BF16)
            return carry

        lax.fori_loop(0, 16, plane_sum, 0, unroll=4)
        own = here[p] * 4 + here[q]
        landing = plane_in.at[a, own]
        for s in PLANE_SHIFTS:
            shift = [0, 0, 0]
            shift[p], shift[q] = s
            there = places.at(shift)
            pltpu.make_async_remote_copy(
                src_ref=line_sum.at[a, there[p] * 4 + there[q]],
                dst_ref=landing,
                send_sem=b_send.at[a],
                recv_sem=b_recv.at[a],
                device_id=places.device(shift),
                device_id_type=MESH,
            ).start()
        plane_in[a, own] = line_sum[a, own]

    for i in range(CHUNKS):
        wait_all(home.at[i], out_recv.at[i])
        pltpu.make_async_copy(back.at[i, me], home.at[i, me], own_sem.at[i]).wait()
    wait_all(straight, r_recv)

    def add(k, acc):
        for n in range(8):
            acc = acc + straight[k * 8 + n].astype(F32)
        return acc

    total_ref[:, 3 * 128 :] = lax.fori_loop(0, CHIPS // 8, add, jnp.zeros((16, 128), F32))
    for a in range(3):
        fifteen(plane_in.at[a], b_recv.at[a])
        value = plane_in[a, 0].astype(F32)
        for k in range(1, 16):
            value = value + plane_in[a, k].astype(F32)
        total_ref[:, a * 128 : (a + 1) * 128] = value

    for n in range(4):
        cross(n).wait_send()
    for i in range(CHUNKS):
        wait_all(sent.at[i], in_send.at[i])
        wait_all(back.at[i], out_send.at[i])
    for a in range(3):
        three(line_in.at[a], a_send.at[a])
        fifteen(plane_in.at[a], b_send.at[a])
    wait_all(straight, r_send)


def finish(home, total, gt, gw, gwo):
    def cells(b, carry):
        p = pl.ds(b, 1)
        blocks = [home[i, p][0].astype(F32) for i in range(CHUNKS)]
        value = jnp.concatenate([unfold(block, NW) for block in blocks], axis=0)
        gt[b // 4, pl.ds(pl.multiple_of((b % 4) * 16, 16), 16)] = value.astype(BF16)
        return carry

    lax.fori_loop(0, home.shape[1], cells, 0, unroll=4)

    @pl.when(pl.program_id(0) == 0)
    def _():
        scaled = total[...] * FACTOR
        for n in range(3):
            gw[:, n * D : (n + 1) * D] = scaled[n * 4 : (n + 1) * 4]
        gwo[...] = scaled[12:]


def body(tokens, cotangent, w_qkv, w_out):
    rows, columns, _ = tokens.shape
    vmem = pltpu.VMEM
    dma = pltpu.SemaphoreType.DMA
    regular = pltpu.SemaphoreType.REGULAR
    home, total = pl.pallas_call(
        kernel,
        out_shape=(
            jax.ShapeDtypeStruct((CHUNKS, CHIPS, 16, OUT_LANES), BF16),
            jax.ShapeDtypeStruct((16, D), F32),
        ),
        in_specs=[pl.BlockSpec(memory_space=pl.ANY)] * 4,
        out_specs=[pl.BlockSpec(memory_space=pl.ANY), pl.BlockSpec(memory_space=vmem)],
        scratch_shapes=[
            vmem((rows, columns, D), BF16),
            vmem((rows, columns, D), BF16),
            vmem((D, 3 * D), BF16),
            vmem((D, D), BF16),
            vmem((CHUNKS, CHIPS, 16, IN_LANES), BF16),
            vmem((CHUNKS, CHIPS, 16, IN_LANES), BF16),
            vmem((4, 2 * ROWS, 128), F32),
            vmem((ROWS, D), F32),
            vmem((ROWS, 128), F32),
            vmem((KEEP * ROWS, D), BF16),
            vmem((KEEP * ROWS, D), BF16),
            vmem((ROWS, 3 * D), BF16),
            vmem((ROWS, D), BF16),
            vmem((KEEP * ROWS, D), BF16),
            vmem((KEEP * ROWS, 3 * D), BF16),
            vmem((ROWS, D), F32),
            vmem((4, ROWS, 128), F32),
            vmem((CHUNKS, CHIPS, 16, OUT_LANES), BF16),
            vmem((D, 4 * D), F32),
            vmem((4, 8, 32, D), BF16),
            vmem((4, 8, 32, D), BF16),
            vmem((4, CHIPS, 16, 128), BF16),
            vmem((3, 4, 16, 16, 128), BF16),
            vmem((3, 16, 16, 128), BF16),
            vmem((3, 16, 16, 128), BF16),
            vmem((CHIPS, 16, 128), BF16),
            dma((4,)), regular, regular, dma((CHUNKS,)),
            dma((CHUNKS,)), dma((CHUNKS,)),
            dma((CHUNKS,)), dma((CHUNKS,)),
            dma((4,)), dma((4,)),
            dma((3,)), dma((3,)),
            dma((3,)), dma((3,)),
            dma(()), dma(()),
        ],
        compiler_params=pltpu.CompilerParams(
            collective_id=0, has_side_effects=True, vmem_limit_bytes=60 << 20
        ),
        name="grid_attention_backward",
    )(tokens, cotangent, w_qkv, w_out)
    steps = 2
    return pl.pallas_call(
        finish,
        grid=(steps,),
        out_shape=(
            jax.ShapeDtypeStruct((rows, columns, D), BF16),
            jax.ShapeDtypeStruct((4, 3 * D), F32),
            jax.ShapeDtypeStruct((4, D), F32),
        ),
        in_specs=[
            pl.BlockSpec((CHUNKS, CHIPS // steps, 16, OUT_LANES), lambda s: (0, s, 0, 0)),
            pl.BlockSpec((16, D), lambda s: (0, 0)),
        ],
        out_specs=[
            pl.BlockSpec((rows // steps, columns, D), lambda s: (s, 0, 0)),
            pl.BlockSpec((4, 3 * D), lambda s: (0, 0)),
            pl.BlockSpec((4, D), lambda s: (0, 0)),
        ],
        compiler_params=pltpu.CompilerParams(vmem_limit_bytes=60 << 20),
        name="cells_from_blocks",
    )(home, total)


def solution(mesh):
    in_specs = (P("gy", "gx", None), P("gy", "gx", None), P(), P())
    out_specs = (P("gy", "gx", None), P(("gy", "gx"), None), P(("gy", "gx"), None))
    return jax.shard_map(body, mesh=mesh, in_specs=in_specs, out_specs=out_specs, check_vma=False)
```
